256 devices in a mesh: wide: 32 (over z_lo, x, core), narrow: 8 (over z_hi, y).
Axes of the slice: x: 4, y: 4, z: 8 (z_hi: 2, z_lo: 4; z = z_hi * 4 + z_lo), core: 2. Of those that a mesh axis runs over, the one named last changes fastest.
Arguments:
- hidden_in: bfloat16 [512, 18432], P('narrow', 'wide'), may hold values from -50 to 50
- ln_gain: float32 [18432], P('wide'), may hold values from 0.5 to 1.5
- gate_weight: bfloat16 [18432, 36864], P('wide', 'narrow'), may hold values from -0.046875 to 0.046875
- up_weight: bfloat16 [18432, 36864], P('wide', 'narrow'), may hold values from -0.046875 to 0.046875
- query_weight: bfloat16 [18432, 6144], P('wide', 'narrow'), may hold values from -0.046875 to 0.046875
- kv_weight: bfloat16 [18432, 512], P('wide'), may hold values from -0.046875 to 0.046875
- out_weight: bfloat16 [6144, 18432], P('narrow', 'wide'), may hold values from -0.078125 to 0.078125
- cache_keys: bfloat16 [512, 384, 256], P(('wide', 'narrow')), may hold values from -130 to 130
- cache_values: bfloat16 [512, 384, 256], P(('wide', 'narrow')), may hold values from -24 to 24
- lengths: int32 [512], P(('wide', 'narrow')), may hold values from 1 to 384, 98304 in all
Outputs:
- update: bfloat16 [512, 18432], P('narrow', 'wide')
- slab_hidden: bfloat16 [512, 36864], P('wide', 'narrow')
The draws below stay inside these ranges and needn't reach their ends.
Inputs may be any that keep to these rules, and one draw needn't show every extreme that they name: `lengths`: the longest request fills all 384 positions in every draw.
All inputs are finite; a program needn't handle non-finite values. No bound on the sum of `lengths` on one device may be relied on, other than what follows from the above.
Results may differ from the reference program's by a relative error of at most 0.012.
Values may be sent and summed in bfloat16 or wider, within the bound.
A program may use at most 128 MiB of HBM per device.

```python
import math
import jax
import jax.numpy as jnp
import numpy as np
from jax import lax

D = 18432
HEADS = 24
HEAD_DIM = 256
SLAB = 36864
CACHE = 384
REQUESTS = 512


def draw_hidden_in(key, part):
    key = jax.random.fold_in(key, 11)
    base_key, row_key, col_key = jax.random.split(key, 3)
    values = jnp.clip(jax.random.normal(base_key, (REQUESTS, D), jnp.float32), -5.0, 5.0)
    row_scale = jnp.exp(jax.random.uniform(row_key, (REQUESTS, 1), jnp.float32, jnp.log(0.3), jnp.log(3.0)))
    column = lax.broadcasted_iota(jnp.float32, (1, D), 1) / D
    rough = jax.random.uniform(col_key, (1, D), jnp.float32, 0.0, 1.0)
    col_scale = jnp.power(10.0, 0.5 * column + 0.5 * rough - 0.5)
    return (values * row_scale * col_scale).astype(jnp.bfloat16)


def draw_cache_keys(key, part):
    key = jax.random.fold_in(key, 23)
    base_key = jax.random.fold_in(key, 0)
    keys = jnp.clip(jax.random.normal(base_key, (REQUESTS, CACHE, HEAD_DIM), jnp.float32), -5.0, 5.0)
    return keys.astype(jnp.bfloat16)


def block_scale(key, dims, cuts, least, top_value):
    gain = 1.0
    for dim, blocks in cuts:
        steps = jax.random.uniform(jax.random.fold_in(jax.random.fold_in(key, 6), dim), (blocks,), jnp.float32, least / len(cuts), top_value / len(cuts))
        gain = gain * jnp.repeat(jnp.exp(steps), dims[dim] // blocks).reshape((-1,) + (1,) * (len(dims) - 1 - dim))
    return gain


def length_profile(amount, total, bound, skew):
    portions = [(1 << 20) // math.isqrt(rank ** skew) + 1 for rank in range(2, amount + 1)]
    surplus, given = total - bound - (amount - 1), [1] * (amount - 1)
    while surplus > 0:
        candidates = [i for i in range(amount - 1) if given[i] < bound]
        pool, left = sum([portions[i] for i in candidates]), surplus
        for i in candidates:
            more = min(bound - given[i], max(1, left * portions[i] // pool), surplus)
            given[i] = given[i] + more
            surplus = surplus - more
    return np.array([bound] + given)


def ragged_sizes(rng, count, total, reach, lean):
    if count == 2:
        one = jax.random.randint(rng, (), max(1, total - reach), min(reach, total - 1) + 1)
        return jnp.stack([one, total - one])
    sizes = jnp.asarray(length_profile(count, total, reach, lean), jnp.int32)
    twos = (count - 1) // 2
    source_of, taker = sizes[1:1 + 2 * twos:2], sizes[2:2 + 2 * twos:2]
    room = jnp.minimum(source_of - 1, reach - taker)
    passed = jax.random.randint(jax.random.fold_in(rng, 1), (twos,), 0, 1 << 20) % (room + 1)
    sizes = sizes.at[1:1 + 2 * twos:2].set(source_of - passed).at[2:2 + 2 * twos:2].set(taker + passed)
    return sizes[jax.random.permutation(jax.random.fold_in(rng, 2), count)]


def noise(rng, shape, width, most, pieces=(), kind=jnp.bfloat16):
    entries = width * jax.random.normal(rng, shape, jnp.float32)
    if pieces:
        entries = entries * block_scale(rng, shape, pieces, -0.22, 0.18)
    return jnp.clip(entries, -most, most).astype(kind)


def setup_inputs(seed: int = 0) -> dict:
    key_list = jax.random.split(jax.random.key(seed), 11)
    return {
        "hidden_in": draw_hidden_in(jax.random.fold_in(key_list[10], 71), 0),
        "ln_gain": jnp.clip(0.5 + 1.0 * jax.random.uniform(key_list[1], (D,), jnp.float32) ** block_scale(key_list[1], (D,), ((0, 32),), -0.2, 0.2), 0.5, 1.5),
        "gate_weight": noise(key_list[2], (D, SLAB), D ** -0.5, 0.046875, ((0, 32), (1, 8))),
        "up_weight": noise(key_list[3], (D, SLAB), D ** -0.5, 0.046875, ((0, 32), (1, 8))),
        "query_weight": noise(key_list[4], (D, HEADS * HEAD_DIM), D ** -0.5, 0.046875, ((0, 32), (1, 8))),
        "kv_weight": noise(key_list[5], (D, 2 * HEAD_DIM), D ** -0.5, 0.046875, ((0, 32),)),
        "out_weight": noise(key_list[6], (HEADS * HEAD_DIM, D), (HEADS * HEAD_DIM) ** -0.5, 0.078125, ((0, 8), (1, 32))),
        "cache_keys": draw_cache_keys(jax.random.fold_in(key_list[10], 71), 0),
        "cache_values": noise(key_list[8], (REQUESTS, CACHE, HEAD_DIM), 4.0, 24.0, ((0, 256),)),
        "lengths": ragged_sizes(key_list[9], REQUESTS, REQUESTS * CACHE // 2, CACHE, 2).astype(jnp.int32),
    }


EPS = 1e-05

def attend(query, new_kv, keys, values, lengths):
    requests = query.shape[0]
    head_dim = keys.shape[2]
    heads = query.shape[1] // head_dim
    grouped = query.reshape(requests, heads, head_dim)
    new_key = new_kv[:, :head_dim]
    new_value = new_kv[:, head_dim:]
    factor = 1.0 / head_dim ** 0.5
    scores = jnp.einsum('rhd,rld->rhl', grouped.astype(jnp.float32), keys.astype(jnp.float32)) * factor
    own_score = jnp.einsum('rhd,rd->rh', grouped.astype(jnp.float32), new_key.astype(jnp.float32)) * factor
    position = lax.broadcasted_iota(jnp.int32, (1, 1, keys.shape[1]), 2)
    usable = position < lengths.astype(jnp.int32)[:, None, None]
    masked = jnp.where(usable, scores, -1e+30)
    highest = jnp.maximum(lax.optimization_barrier(jnp.max(masked, axis=2)), own_score)
    exps = jnp.where(usable, jnp.exp(masked - highest[:, :, None]), 0.0)
    own_exp = jnp.exp(own_score - highest)
    denominator = lax.optimization_barrier(jnp.sum(exps, axis=2)) + own_exp
    cached_weights = (exps / denominator[:, :, None]).astype(jnp.bfloat16)
    own_weight = (own_exp / denominator).astype(jnp.bfloat16)
    context = jnp.einsum('rhl,rld->rhd', cached_weights.astype(jnp.float32), values.astype(jnp.float32))
    context = context + own_weight.astype(jnp.float32)[:, :, None] * new_value.astype(jnp.float32)[:, None, :]
    return context.reshape(requests, heads * head_dim).astype(jnp.bfloat16)

def blocked(normed, weight):
    return jnp.dot(normed, weight, preferred_element_type=jnp.float32)

def reference(hidden_in, ln_gain, gate_weight, up_weight, query_weight, kv_weight, out_weight, cache_keys, cache_values, lengths):
    floats = hidden_in.astype(jnp.float32)
    row_average = lax.optimization_barrier(jnp.mean(floats, axis=1, keepdims=True))
    row_variance = lax.optimization_barrier(jnp.mean(floats * floats, axis=1, keepdims=True)) - row_average * row_average
    normed = ((floats - row_average) * lax.rsqrt(row_variance + EPS) * ln_gain.astype(jnp.float32)[None, :]).astype(jnp.bfloat16)
    gate = blocked(normed, gate_weight)
    up_full = blocked(normed, up_weight)
    query_full = blocked(normed, query_weight)
    kv_full = blocked(normed, kv_weight)
    slab_hidden = (jax.nn.silu(gate) * up_full).astype(jnp.bfloat16)
    query = query_full.astype(jnp.bfloat16)
    new_kv = kv_full.astype(jnp.bfloat16)
    group_size = 16
    groups = REQUESTS // group_size

    def attend_group(items):
        return attend(items[0], items[1], items[2], items[3], items[4])
    context = lax.map(attend_group, (query.reshape(groups, group_size, query.shape[1]), new_kv.reshape(groups, group_size, new_kv.shape[1]), cache_keys.reshape(groups, group_size, CACHE, HEAD_DIM), cache_values.reshape(groups, group_size, CACHE, HEAD_DIM), lengths.reshape(groups, group_size)))
    context = context.reshape(REQUESTS, HEADS * HEAD_DIM)
    attention = jnp.dot(context, out_weight, preferred_element_type=jnp.float32)
    return (attention.astype(jnp.bfloat16), slab_hidden)
```

```python
import functools

import jax
import jax.numpy as jnp
from jax import lax
from jax.experimental import pallas as pl
from jax.experimental.pallas import tpu as pltpu
from jax.sharding import PartitionSpec as P

D = 18432
EPS = 1e-05
MESH = pl.DeviceIdType.MESH
F32 = jnp.float32
BF16 = jnp.bfloat16
KB = 576
KP = 640
CHUNKS = 9
CW = 256
HALF = CHUNKS * CW

STEP = dict(Q1=2, Q2=5, Q3=6, Q4=7, C1=9, C2=10, C3=12, C4=13, C5=15)
LAG1, LAG2, LAG3 = 2, 4, 6
STEPS = 16


def device(x, y, zl, zh, c):
    return ((zl * 4 + x) * 2 + c, zh * 4 + y)


def kernel(
    hidden,
    gain,
    gate_w,
    up_w,
    query_w,
    kv_w,
    out_w,
    keys_h,
    values_h,
    lengths,
    update,
    slab,
    raw,
    normed,
    gains,
    wgu,
    wq,
    wkv,
    wo,
    keys,
    values,
    cst,
    zst,
    xst,
    yst,
    part,
    r1,
    s1,
    r2,
    zs,
    zr,
    sl,
    sr,
    kvs,
    pq,
    rq,
    zq,
    zqr,
    cx,
    cxr,
    yt,
    yr,
    q48,
    ctx,
    caf,
    ca,
    ar,
    bs,
    br,
    brf,
    ctf,
    ct,
    os_,
    or_,
    vf,
    fs,
    fr,
    lsem,
    wS, wR, gS, gR, rawS, rawR, sibS, sibR,
    cstS, cstR, zstS, zstR, xstS, xstR, ystS, ystR,
    r1S, r1R, r2S, r2R, zS, zR, slS, slR,
    qxS, qxR, qzS, qzR, qcS, qcR, qyS, qyR,
    aS, aR, bS, bR, cS, cR, dS, dR, eS, eR, fS, fR,
):
    w = lax.axis_index("wide")
    n = lax.axis_index("narrow")
    c = lax.rem(w, 2)
    x = lax.rem(w // 2, 4)
    zl = w // 8
    zh = n // 4
    y = lax.rem(n, 4)
    z = zh * 4 + zl
    sib = device(x, y, zl, zh, 1 - c)
    partner = device(x, y, zl, 1 - zh, c)

    def on_x(p):
        return device(p, y, zl, zh, c)

    def on_y(p):
        return device(x, p, zl, zh, c)

    def on_z(p):
        return device(x, y, lax.rem(p, 4), p // 4, c)

    def remote(src, dst, ss, rs, to):
        return pltpu.make_async_remote_copy(
            src_ref=src, dst_ref=dst, send_sem=ss, recv_sem=rs, device_id=to, device_id_type=MESH
        )

    drains = {}

    def start(name, args):
        remote(*args()).start()
        drains[name] = lambda: remote(*args()).wait_send()

    def arrived(dst, ss, rs):
        remote(dst, dst, ss, rs, sib).wait_recv()

    def peers(me, size):
        return [(d, lax.rem(me + d, size)) for d in range(1, size)]

    on_x.peers, on_y.peers, on_z.peers = peers(x, 4), peers(y, 4), peers(z, 8)
    zl_peers = peers(zl, 4)

    def spread(name, src, dst, ss, rs, me, on):
        for d, p in on.peers:
            start(name + str(d), lambda d=d, p=p: (src(p), dst.at[me], ss.at[d], rs.at[me], on(p)))

    def collect(dst, ss, rs, on):
        for d, p in on.peers:
            arrived(dst.at[p], ss.at[d], rs.at[p])

    half = pl.multiple_of(c * HALF, 128)
    other = pl.multiple_of((1 - c) * HALF, 128)
    mine = pl.ds(pl.multiple_of(c * KP, 128), KB)

    def local(src, dst, i):
        return pltpu.make_async_copy(src, dst, lsem.at[i])

    load_x = local(hidden, raw.at[c, n], 0)
    load_x.start()
    load_q = local(query_w.at[:, pl.ds(pl.multiple_of(c * 384, 128), 384)], wq.at[mine], 1)
    load_kv = local(kv_w.at[:, pl.ds(pl.multiple_of(c * 256, 128), 256)], wkv.at[mine], 2)
    load_o = local(out_w, wo, 3)
    load_k = local(keys_h, keys, 4)
    load_v = local(values_h, values, 5)
    load_q.start()
    load_kv.start()

    def load_gu(j, k):
        src = (gate_w, up_w)[k].at[:, pl.ds(pl.multiple_of(half + j * CW, 128), CW)]
        return local(src, wgu.at[j, mine, pl.ds(k * CW, CW)], 6 + 2 * j + k)

    def send_gu(j, k):
        src = (gate_w, up_w)[k].at[:, pl.ds(pl.multiple_of(other + j * CW, 128), CW)]
        i = 2 + 2 * j + k
        return remote(src, wgu.at[j, mine, pl.ds(k * CW, CW)], wS.at[i], wR.at[i], sib)

    barrier = pltpu.get_barrier_semaphore()
    greeted = (
        [sib]
        + [on_x(p) for _, p in on_x.peers]
        + [on_y(p) for _, p in on_y.peers]
        + [on_z(p) for _, p in on_z.peers]
    )
    for to in greeted:
        pl.semaphore_signal(barrier, inc=1, device_id=to, device_id_type=MESH)

    load_x.wait()
    own = raw[c, n].astype(F32)
    lane = lax.broadcasted_iota(jnp.int32, (64, 128), 1)
    cst[c] = jnp.where(
        lane < 64,
        jnp.sum(own, axis=1, keepdims=True),
        jnp.sum(own * own, axis=1, keepdims=True),
    )
    g8 = jnp.broadcast_to(gain[...], (8, KB))
    gains[c] = g8

    pl.semaphore_wait(barrier, len(greeted))

    start("b11", lambda: (cst.at[c], cst.at[c], cstS.at[0], cstR.at[0], sib))
    for d, p in on_y.peers:
        start("b12_" + str(d), lambda d=d, p=p: (raw.at[c, n], raw.at[c, n], rawS.at[d], rawR.at[n], on_y(p)))
    start("b13", lambda: (raw.at[c, n], raw.at[c, n], rawS.at[0], rawR.at[n], partner))
    start("b14", lambda: (gains.at[c], gains.at[c], gS.at[0], gR.at[0], sib))
    away_q = pl.ds(pl.multiple_of((1 - c) * 384, 128), 384)
    away_kv = pl.ds(pl.multiple_of((1 - c) * 256, 128), 256)
    start("wq", lambda: (query_w.at[:, away_q], wq.at[mine], wS.at[0], wR.at[0], sib))
    start("wkv", lambda: (kv_w.at[:, away_kv], wkv.at[mine], wS.at[1], wR.at[1], sib))

    arrived(cst.at[1 - c], cstS.at[0], cstR.at[0])
    zst[z] = cst[0] + cst[1]
    spread("a01_", lambda p: zst.at[z], zst, zstS, zstR, z, on_z)

    def start_weights(j, carry):
        for k in range(2):
            send_gu(j, k).start()
            load_gu(j, k).start()
        return carry

    lax.fori_loop(0, CHUNKS, start_weights, 0)
    load_o.start()
    load_k.start()
    load_v.start()

    for k in range(2):
        pad = pl.ds(k * KP + KB, KP - KB)
        normed[:, pad] = jnp.zeros((512, KP - KB), BF16)
        wq[pad, :] = jnp.zeros((KP - KB, 384), BF16)
        wkv[pad, :] = jnp.zeros((KP - KB, 256), BF16)

        def fill(j, carry, pad=pad):
            wgu[j, pad, :] = jnp.zeros((KP - KB, 2 * CW), BF16)
            return carry

        lax.fori_loop(0, CHUNKS, fill, 0)
    pq[:, :, 32:40, :] = jnp.zeros((4, 4, 8, 384), F32)
    caf[...] = jnp.zeros((2, 32, 256), F32)

    far = (1 - zh) * 4 + y
    arrived(raw.at[c, far], rawS.at[0], rawR.at[far])
    for d, p in on_y.peers:
        start("b15_" + str(d), lambda d=d, p=p: (raw.at[c, far], raw.at[c, far], rawS.at[3 + d], rawR.at[far], on_y(p)))
    collect(zst, zstS, zstR, on_z)
    for k in range(2):
        xst[x, k] = (zst[4 * k] + zst[4 * k + 1]) + (zst[4 * k + 2] + zst[4 * k + 3])
    spread("a02_", lambda p: xst.at[x], xst, xstS, xstR, x, on_x)
    for d, p in on_y.peers:
        arrived(raw.at[c, zh * 4 + p], rawS.at[d], rawR.at[zh * 4 + p])
    near4 = pl.ds(zh * 4, 4)
    far4 = pl.ds((1 - zh) * 4, 4)
    start("b16", lambda: (raw.at[c, near4], raw.at[c, near4], sibS.at[0], sibR.at[0], sib))
    collect(xst, xstS, xstR, on_x)
    yst[y] = (xst[0] + xst[1]) + (xst[2] + xst[3])
    spread("a03_", lambda p: yst.at[y], yst, ystS, ystR, y, on_y)
    for d, p in on_y.peers:
        arrived(raw.at[c, (1 - zh) * 4 + p], rawS.at[3 + d], rawR.at[(1 - zh) * 4 + p])
    start("b17", lambda: (raw.at[c, far4], raw.at[c, far4], sibS.at[1], sibR.at[1], sib))
    arrived(gains.at[1 - c], gS.at[0], gR.at[0])
    collect(yst, ystS, ystR, on_y)
    arrived(raw.at[1 - c, near4], sibS.at[0], sibR.at[0])
    arrived(raw.at[1 - c, far4], sibS.at[1], sibR.at[1])

    def norm(b, carry):
        stat = yst[lax.rem(b, 4), b // 4]
        average = stat[:, 0:1] / D
        variance = stat[:, 64:65] / D - average * average
        scale = lax.rsqrt(variance + EPS)
        rows = pl.ds(pl.multiple_of(b * 64, 64), 64)
        for k in range(2):
            block = (raw[k, b].astype(F32) - average) * scale * gains[k, 0:1, :]
            normed[rows, k * KP : k * KP + KB] = block.astype(BF16)
        return carry

    lax.fori_loop(0, 8, norm, 0)

    load_q.wait()
    load_kv.wait()
    arrived(wq.at[mine], wS.at[0], wR.at[0])
    arrived(wkv.at[mine], wS.at[1], wR.at[1])
    query = jnp.dot(normed[...], wq[...], preferred_element_type=F32)
    for zz in range(4):
        for xx in range(4):
            at = zz * 128 + xx * 32
            pq[xx, zz, 0:32, :] = query[at : at + 32]
    k64 = lax.broadcasted_iota(jnp.int32, (64, 512), 0)
    r512 = lax.broadcasted_iota(jnp.int32, (64, 512), 1)
    pick = r512 == (k64 >> 1) * 16 + n * 2 + (k64 & 1)
    chosen = jnp.dot(
        jnp.where(pick, 1.0, 0.0).astype(BF16), normed[...], preferred_element_type=F32
    ).astype(BF16)
    kvs[...] = jnp.dot(chosen, wkv[...], preferred_element_type=F32)
    for zz in range(4):
        for xx in range(4):
            at = zz * 16 + xx * 4
            pq[xx, zz, 32:36, 0:256] = kvs[at : at + 4, :]
    spread("a04_", lambda p: pq.at[p], rq, qxS, qxR, x, on_x)

    def part_q1():
        collect(rq, qxS, qxR, on_x)
        total = pq[x]
        for _, p in on_x.peers:
            total = total + rq[p]
        for zz in range(4):
            for hh in range(2):
                to = hh * 4 + zz
                zq[to, 0:8] = total[zz, hh * 8 : hh * 8 + 8]
                zq[to, 8:16] = total[zz, 16 + hh * 8 : 24 + hh * 8]
                zq[to, 16:24] = total[zz, 32:40]
        zqr[z] = zq[z]
        spread("a05_", lambda p: zq.at[p], zqr, qzS, qzR, z, on_z)

    def part_q2():
        collect(zqr, qzS, qzR, on_z)
        sums = [(zqr[k] + zqr[k + 1]) + (zqr[k + 2] + zqr[k + 3]) for k in (0, 4)]
        new = jnp.where(zh == 0, sums[0][16:24], sums[1][16:24])
        for cc in range(2):
            cx[cc, 0:8] = sums[0][cc * 8 : cc * 8 + 8]
            cx[cc, 8:16] = sums[1][cc * 8 : cc * 8 + 8]
            cx[cc, 16:24] = new
        cxr[c] = cx[c]
        start("b18", lambda: (cx.at[1 - c], cxr.at[c], qcS.at[0], qcR.at[0], sib))

    def part_q3():
        arrived(cxr.at[1 - c], qcS.at[0], qcR.at[0])
        for yy in range(4):
            for cs in range(2):
                for hs in range(2):
                    at = hs * 8 + yy * 2
                    yt[yy, cs * 4 + hs * 2 : cs * 4 + hs * 2 + 2, :] = cxr[cs, at : at + 2, :]
        yr[y] = yt[y]
        spread("a06_", lambda p: yt.at[p], yr, qyS, qyR, y, on_y)

    def part_q4():
        collect(yr, qyS, qyR, on_y)
        for yy in range(4):
            at = yy * 4
            q48[at : at + 4, :] = yr[yy, 0:4, 0:256]
            q48[16 + at : 20 + at, 0:128] = yr[yy, 0:4, 256:384]
            q48[16 + at : 20 + at, 128:256] = yr[yy, 4:8, 0:128]
            q48[32 + at : 36 + at, :] = yr[yy, 4:8, 128:384]
        load_k.wait()
        load_v.wait()
        q = q48[...].astype(BF16)
        factor = 1.0 / 16.0
        first = lax.broadcasted_iota(jnp.int32, (48, 1), 0) % 2 == 0

        def fresh(k):
            pair = jnp.where(c == 0, cxr[k, 16:18, 0:256], cxr[k, 18:20, 0:256])
            pair = pair.astype(BF16).astype(F32)
            return jnp.where(first, pair[0:1, :], pair[1:2, :])

        def scores_of(r):
            return lax.dot_general(q, keys[r], (((1,), (1,)), ((), ())), preferred_element_type=F32)

        scores = jnp.where(first, scores_of(0), scores_of(1)) * factor
        own_score = jnp.sum(q.astype(F32) * fresh(0), axis=1, keepdims=True) * factor
        position = lax.broadcasted_iota(jnp.int32, (48, 384), 1)
        usable = position < jnp.where(first, lengths[0], lengths[1])
        masked = jnp.where(usable, scores, -1e30)
        highest = jnp.maximum(jnp.max(masked, axis=1, keepdims=True), own_score)
        exps = jnp.where(usable, jnp.exp(masked - highest), 0.0)
        own_exp = jnp.exp(own_score - highest)
        denominator = jnp.sum(exps, axis=1, keepdims=True) + own_exp
        weights = (exps / denominator).astype(BF16)
        own_weight = (own_exp / denominator).astype(BF16).astype(F32)

        def mixed(r):
            return jnp.dot(weights, values[r], preferred_element_type=F32)

        context = jnp.where(first, mixed(0), mixed(1)) + own_weight * fresh(1)
        ctx[...] = context
        for t in range(3):
            for yy in range(4):
                for hh in range(2):
                    at = t * 16 + yy * 4 + hh * 2
                    caf[hh, yy * 8 + t * 2 : yy * 8 + t * 2 + 2, :] = ctx[at : at + 2, :]
        ca[...] = caf[...].astype(BF16)
        ar[z] = ca[zh]
        spread("a07_", lambda p: ca.at[p // 4], ar, aS, aR, z, on_z)

    def part_c1():
        collect(ar, aS, aR, on_z)
        for yy in range(4):
            bs[yy] = ar[:, yy * 8 : yy * 8 + 8, :].astype(F32).reshape(64, 256).astype(BF16)
        br[y] = bs[y]
        spread("a08_", lambda p: bs.at[p], br, bS, bR, y, on_y)

    def part_c2():
        collect(br, bS, bR, on_y)
        brf[...] = br[...].astype(F32)
        for t in range(3):
            for zz in range(4):
                for hh in range(2):
                    for yy in range(4):
                        to = zz * 16 + hh * 8 + yy * 2
                        at = (hh * 4 + zz) * 8 + t * 2
                        ctf[to : to + 2, t * 256 : t * 256 + 256] = brf[yy, at : at + 2, :]
        ct[c, x] = ctf[...].astype(BF16)
        for d, p in on_x.peers:
            start("b19_" + str(d), lambda d=d, p=p: (ct.at[c, x], ct.at[c, x], cS.at[d], cR.at[x], on_x(p)))
        start("b20", lambda: (ct.at[c, x], ct.at[c, x], dS.at[0], dR.at[x], sib))

    def part_c3():
        for d, p in on_x.peers:
            arrived(ct.at[c, p], cS.at[d], cR.at[p])
            start("b21_" + str(d), lambda d=d, p=p: (ct.at[c, p], ct.at[c, p], dS.at[d], dR.at[p], sib))

    def part_c4():
        load_o.wait()
        for p in range(4):
            arrived(ct.at[1 - c, p], dS.at[p], dR.at[p])
        out = jnp.dot(ct[...].reshape(512, 768), wo[...], preferred_element_type=F32)
        for cc in range(2):
            for xx in range(4):
                for zz in range(4):
                    at = cc * 256 + xx * 64 + zz * 16
                    to = (xx % 2) * 32 + cc * 16
                    os_[(zz % 2) * 2 + xx // 2, zz // 2, to : to + 16, :] = out[at : at + 16].astype(
                        BF16
                    )
        spread("a09_", lambda p: os_.at[p], or_, eS, eR, y, on_y)

    def part_c5():
        collect(or_, eS, eR, on_y)
        total = os_[y].astype(F32)
        for _, p in on_y.peers:
            total = total + or_[p].astype(F32)
        vf[...] = total
        fs[...] = total.astype(BF16)
        start("b22", lambda: (fs.at[1 - zh], fr, fS.at[0], fR.at[0], partner))

    right, left = lax.rem(x + 1, 4), lax.rem(x + 3, 4)
    across = lax.rem(x + 2, 4)

    def first_copies(j):
        return [
            remote(
                part.at[j, :, across, :, pl.ds(k * CW, CW)],
                r1.at[j, k], r1S.at[j, k], r1R.at[j, k], on_x(to),
            )
            for k, to in enumerate((right, left))
        ]

    def second_copies(j):
        return [
            remote(s1.at[j, k], r2.at[j, k], r2S.at[j, k], r2R.at[j, k], on_x(to))
            for k, to in enumerate((right, left))
        ]

    def third_copies(j):
        return [
            remote(zs.at[j, p], zr.at[j, zl], zS.at[j, d], zR.at[j, zl], device(x, y, p, zh, c))
            for d, p in zl_peers
        ]

    def last_copy(j):
        return remote(sl.at[j, 1 - c], sr.at[j], slS.at[j], slR.at[j], sib)

    def multiply(j):
        for k in range(2):
            load_gu(j, k).wait()
            send_gu(j, k).wait_recv()
        product = jnp.dot(normed[...], wgu[j], preferred_element_type=F32)
        part[j] = product.astype(BF16).reshape(4, 4, 32, 2 * CW)
        for copy in first_copies(j):
            copy.start()

    def add_first(j):
        for copy in first_copies(j):
            copy.wait_recv()
        for k, to in enumerate((right, left)):
            for m in range(2):
                cols = slice(m * CW, m * CW + CW)
                if m == k:
                    total = part[j, :, to, :, cols].astype(F32) + r1[j, k].astype(F32)
                    s1[j, k, :, :, cols] = total.astype(BF16)
                else:
                    s1[j, k, :, :, cols] = part[j, :, to, :, cols]
        for copy in second_copies(j):
            copy.start()

    def add_second(j):
        for copy in second_copies(j):
            copy.wait_recv()
        total = part[j, :, x].astype(F32) + r2[j, 0].astype(F32) + r2[j, 1].astype(F32)
        zs[j] = total.astype(BF16)
        for copy in third_copies(j):
            copy.start()

    def finish(j):
        for d, p in zl_peers:
            arrived(zr.at[j, p], zS.at[j, d], zR.at[j, p])
        total = zs[j, zl].astype(F32)
        for _, p in zl_peers:
            total = total + zr[j, p].astype(F32)
        g = total[:, :CW]
        hidden_units = (g * (1.0 / (1.0 + jnp.exp(-g))) * total[:, CW:]).astype(BF16)
        sl[j] = hidden_units.reshape(2, 16, CW)
        last_copy(j).start()
        slab[:, pl.ds(pl.multiple_of(half + j * CW, 128), CW)] = sl[j, c]

    parts = dict(
        Q1=part_q1, Q2=part_q2, Q3=part_q3, Q4=part_q4,
        C1=part_c1, C2=part_c2, C3=part_c3, C4=part_c4, C5=part_c5,
    )

    def step(k, carry):
        for name, run in parts.items():
            pl.when(k == STEP[name])(run)
        for lag, run in ((LAG3, finish), (LAG2, add_second), (LAG1, add_first), (0, multiply)):
            j = k - lag
            pl.when(jnp.logical_and(j >= 0, j < CHUNKS))(functools.partial(run, j))
        return carry

    lax.fori_loop(0, STEPS, step, 0)

    def rest(j, carry):
        last_copy(j).wait_recv()
        slab[:, pl.ds(pl.multiple_of(other + j * CW, 128), CW)] = sr[j]
        for copy in first_copies(j) + second_copies(j) + third_copies(j) + [last_copy(j)]:
            copy.wait_send()
        for k in range(2):
            send_gu(j, k).wait_send()
        return carry

    lax.fori_loop(0, CHUNKS, rest, 0)
    arrived(fr, fS.at[0], fR.at[0])
    update[...] = (vf[zh] + fr[...].astype(F32)).astype(BF16)
    for drain in drains.values():
        drain()


def scratch():
    v = pltpu.VMEM
    s = lambda *shape: pltpu.SemaphoreType.DMA(shape)
    buffers = [
        v((2, 8, 64, KB), BF16),
        v((512, 2 * KP), BF16),
        v((2, 8, KB), F32),
        v((CHUNKS, 2 * KP, 2 * CW), BF16),
        v((2 * KP, 384), BF16),
        v((2 * KP, 256), BF16),
        v((768, KB), BF16),
        v((2, 384, 256), BF16),
        v((2, 384, 256), BF16),
        v((2, 64, 128), F32),
        v((8, 64, 128), F32),
        v((4, 2, 64, 128), F32),
        v((4, 2, 64, 128), F32),
        v((CHUNKS, 4, 4, 32, 2 * CW), BF16),
        v((CHUNKS, 2, 4, 32, CW), BF16),
        v((CHUNKS, 2, 4, 32, 2 * CW), BF16),
        v((CHUNKS, 2, 4, 32, 2 * CW), BF16),
        v((CHUNKS, 4, 32, 2 * CW), BF16),
        v((CHUNKS, 4, 32, 2 * CW), BF16),
        v((CHUNKS, 2, 16, CW), BF16),
        v((CHUNKS, 16, CW), BF16),
        v((64, 256), F32),
        v((4, 4, 40, 384), F32),
        v((4, 4, 40, 384), F32),
        v((8, 24, 384), F32),
        v((8, 24, 384), F32),
        v((2, 24, 384), F32),
        v((2, 24, 384), F32),
        v((4, 8, 384), F32),
        v((4, 8, 384), F32),
        v((48, 256), F32),
        v((48, 256), F32),
        v((2, 32, 256), F32),
        v((2, 32, 256), BF16),
        v((8, 32, 256), BF16),
        v((4, 64, 256), BF16),
        v((4, 64, 256), BF16),
        v((4, 64, 256), F32),
        v((64, 768), F32),
        v((2, 4, 64, 768), BF16),
        v((4, 2, 64, KB), BF16),
        v((4, 2, 64, KB), BF16),
        v((2, 64, KB), F32),
        v((2, 64, KB), BF16),
        v((64, KB), BF16),
    ]
    pair = lambda *shape: [s(*shape), s(*shape)]
    sems = [s(6 + 2 * CHUNKS)]
    sems += pair(2 + 2 * CHUNKS) + pair(1) + [s(7), s(8)] + pair(2)
    sems += pair(1) + pair(8) + pair(4) + pair(4)
    sems += pair(CHUNKS, 2) + pair(CHUNKS, 2) + pair(CHUNKS, 4) + pair(CHUNKS)
    sems += pair(4) + pair(8) + pair(1) + pair(4)
    sems += pair(8) + pair(4) + pair(4) + pair(4) + pair(4) + pair(1)
    return buffers + sems


def local(hidden, gain, *rest):
    anywhere = pl.BlockSpec(memory_space=pl.ANY)
    vmem = pl.BlockSpec(memory_space=pltpu.VMEM)
    return pl.pallas_call(
        kernel,
        out_shape=(
            jax.ShapeDtypeStruct((64, KB), BF16),
            jax.ShapeDtypeStruct((16, 2 * HALF), BF16),
        ),
        in_specs=[anywhere, vmem] + [anywhere] * 7 + [pl.BlockSpec(memory_space=pltpu.SMEM)],
        out_specs=(vmem, vmem),
        scratch_shapes=scratch(),
        compiler_params=pltpu.CompilerParams(
            collective_id=0, has_side_effects=True, vmem_limit_bytes=58 * 1024 * 1024
        ),
        name="layer",
    )(hidden, gain.reshape(1, KB), *rest)


def solution(mesh):
    placed = (
        P("narrow", "wide"),
        P("wide"),
        P("wide", "narrow"),
        P("wide", "narrow"),
        P("wide", "narrow"),
        P("wide", None),
        P("narrow", "wide"),
        P(("wide", "narrow"), None, None),
        P(("wide", "narrow"), None, None),
        P(("wide", "narrow")),
    )
    return jax.shard_map(
        local,
        mesh=mesh,
        in_specs=placed,
        out_specs=(P("narrow", "wide"), P("wide", "narrow")),
        check_vma=False,
    )
```

```python
import functools

import jax
import jax.numpy as jnp
from jax import lax
from jax.experimental import pallas as pl
from jax.experimental.pallas import tpu as pltpu
from jax.sharding import PartitionSpec as P

D = 18432
EPS = 1e-05
MESH = pl.DeviceIdType.MESH
F32 = jnp.float32
BF16 = jnp.bfloat16
KB = 576
KP = 640
CHUNKS = 9
CW = 256
HALF = CHUNKS * CW

STEP = dict(Q1=2, Q2=5, Q4=7, C1=8, C2=9, C4=11, C5=13)
LAG1, LAG2, LAG3 = 2, 4, 6
Z_LAG1, Z_LAG2 = 4, 7
Z_FIRST = (0,)
STEPS = 16


def device(x, y, zl, zh, c):
    return ((zl * 4 + x) * 2 + c, zh * 4 + y)


def kernel(
    hidden,
    gain,
    gate_w,
    up_w,
    query_w,
    kv_w,
    out_w,
    keys_h,
    values_h,
    lengths,
    update,
    slab,
    raw,
    normed,
    gains,
    wgu,
    wq,
    wkv,
    wo,
    keys,
    values,
    cst,
    zst,
    xst,
    yst,
    part,
    r1,
    s1,
    r2,
    zs,
    zr,
    zb,
    xs,
    xr,
    sl,
    sr,
    kvs,
    kvp,
    kvr,
    kz,
    kzr,
    kc,
    pq,
    rq,
    zq,
    zqr,
    cx,
    yt,
    yr,
    q48,
    ctx,
    caf,
    ca,
    ar,
    bs,
    br,
    brf,
    ctf,
    ct,
    os_,
    or_,
    vf,
    fs,
    fr,
    gs,
    gr,
    lsem,
    sent,
    come,
    chunk_w,
    chunk_1,
    chunk_2,
    chunk_3,
):
    w = lax.axis_index("wide")
    n = lax.axis_index("narrow")
    c = lax.rem(w, 2)
    x = lax.rem(w // 2, 4)
    zl = w // 8
    zh = n // 4
    y = lax.rem(n, 4)
    z = zh * 4 + zl
    oc = 1 - c
    sib = device(x, y, zl, zh, 1 - c)
    partner = device(x, y, zl, 1 - zh, c)
    partner_sib = device(x, y, zl, 1 - zh, oc)

    def on_x(p):
        return device(p, y, zl, zh, c)

    def on_y(p):
        return device(x, p, zl, zh, c)

    def on_y_sib(p):
        return device(x, p, zl, zh, oc)

    def on_z(p):
        return device(x, y, lax.rem(p, 4), p // 4, c)

    def remote(src, dst, ss, rs, to):
        return pltpu.make_async_remote_copy(
            src_ref=src, dst_ref=dst, send_sem=ss, recv_sem=rs, device_id=to, device_id_type=MESH
        )

    def peers(me, size):
        return [(d, lax.rem(me + d, size)) for d in range(1, size)]

    on_x.peers, on_y.peers, on_z.peers = peers(x, 4), peers(y, 4), peers(z, 8)
    zl_peers = peers(zl, 4)

    def on_zl(p):
        return device(x, y, p, zh, c)

    on_zl.peers = zl_peers

    names = (
        "cst", "zst", "xst", "yst", "gain", "near", "zh0", "zh1", "far0", "far1", "sib0", "sib1", "sib2", "wq", "wkv",
        "wo", "qx", "kx", "qz", "kz", "kc", "qy", "a", "b", "c", "e0", "e1", "f", "g",
        "last",
    )
    slot = {name: i for i, name in enumerate(names)}

    def start(name, src, dst, to):
        remote(src, dst, sent.at[slot[name]], come.at[slot[name]], to).start()

    def arrive(name, dst):
        remote(dst, dst, sent.at[slot[name]], come.at[slot[name]], sib).wait_recv()

    def spread(name, src, dst, me, on):
        for _, p in on.peers:
            start(name, src(p), dst.at[me], on(p))

    def collect(name, dst, on):
        arrive(name, dst.at[pl.ds(0, len(on.peers))])

    half = pl.multiple_of(c * HALF, 128)
    other = pl.multiple_of((1 - c) * HALF, 128)
    mine = pl.ds(pl.multiple_of(c * KP, 128), KB)

    def local(src, dst, i):
        return pltpu.make_async_copy(src, dst, lsem.at[i])

    load_x = local(hidden, raw.at[c, n], 0)
    load_x.start()
    load_q = local(query_w.at[:, pl.ds(pl.multiple_of(c * 384, 128), 384)], wq.at[mine], 1)
    load_kv = local(kv_w.at[:, pl.ds(pl.multiple_of(c * 256, 128), 256)], wkv.at[mine], 2)
    load_o = local(out_w, wo.at[c], 3)
    load_k = local(keys_h, keys, 4)
    load_v = local(values_h, values, 5)
    load_q.start()
    load_kv.start()

    barrier = pltpu.get_barrier_semaphore()
    greeted = [on(p) for on in (on_z, on_x, on_y) for _, p in on.peers] + [sib]
    greeted += [on_y_sib(p) for _, p in on_y.peers] + [partner_sib]
    for to in greeted:
        pl.semaphore_signal(barrier, inc=1, device_id=to, device_id_type=MESH)

    for k in range(2):
        pad = pl.ds(k * KP + KB, KP - KB)
        normed[:, pad] = jnp.zeros((512, KP - KB), BF16)
        wq[pad, :] = jnp.zeros((KP - KB, 384), BF16)
        wkv[pad, :] = jnp.zeros((KP - KB, 256), BF16)

        def fill(j, carry, pad=pad):
            wgu[j, pad, :] = jnp.zeros((KP - KB, 2 * CW), BF16)
            return carry

        lax.fori_loop(0, CHUNKS, fill, 0)
    caf[...] = jnp.zeros((2, 32, 256), F32)
    yt[...] = jnp.zeros((2, 4, 8, 384), F32)
    load_x.wait()
    own = raw[c, n].astype(F32)
    row64 = lax.broadcasted_iota(jnp.int32, (64, 128), 0)
    lane = lax.broadcasted_iota(jnp.int32, (64, 128), 1)
    both = jnp.where(
        lane < 64,
        jnp.sum(own, axis=1, keepdims=True),
        jnp.sum(own * own, axis=1, keepdims=True),
    )
    line = jnp.sum(jnp.where((lane & 63) == row64, both, 0.0), axis=0, keepdims=True)
    cst[c] = jnp.broadcast_to(line, (8, 128))
    gains[c] = jnp.broadcast_to(gain[...].reshape(1, KB), (8, KB))

    pl.semaphore_wait(barrier, len(greeted))

    start("cst", cst.at[c], cst.at[c], sib)
    top = [pl.ds(0, 32), pl.ds(32, 32)]
    for i in range(2):
        start(f"zh{i}", raw.at[c, n, top[i]], raw.at[c, n, top[i]], partner)
    for _, p in on_y.peers:
        start("near", raw.at[c, n], raw.at[c, n], on_y(p))
    start("gain", gains.at[c], gains.at[c], sib)
    arrive("cst", cst.at[oc])
    zst[z] = cst[0] + cst[1]
    spread("zst", lambda p: zst.at[z], zst, z, on_z)
    away_q = pl.ds(pl.multiple_of((1 - c) * 384, 128), 384)
    away_kv = pl.ds(pl.multiple_of((1 - c) * 256, 128), 256)
    start("wq", query_w.at[:, away_q], wq.at[mine], sib)
    start("wkv", kv_w.at[:, away_kv], wkv.at[mine], sib)

    def start_weights(j, carry):
        g = j // 3
        for k, weight in enumerate((gate_w, up_w)):
            to = wgu.at[j, mine, pl.ds(k * CW, CW)]
            there = weight.at[:, pl.ds(pl.multiple_of(other + j * CW, 128), CW)]
            remote(there, to, chunk_w.at[0], chunk_w.at[1 + g], sib).start()
            here = weight.at[:, pl.ds(pl.multiple_of(half + j * CW, 128), CW)]
            local(here, to, 6 + g).start()
        return carry

    lax.fori_loop(0, CHUNKS, start_weights, 0)
    start("wo", out_w, wo.at[c], sib)
    load_o.start()
    load_k.start()
    load_v.start()

    far = (1 - zh) * 4 + y
    near4 = pl.ds(zh * 4, 4)
    far4 = pl.ds((1 - zh) * 4, 4)
    collect("zst", zst, on_z)
    upper = lax.broadcasted_iota(jnp.int32, (8, 128), 0) < 4
    xst[x] = jnp.where(
        upper, (zst[0] + zst[1]) + (zst[2] + zst[3]), (zst[4] + zst[5]) + (zst[6] + zst[7])
    )
    spread("xst", lambda p: xst.at[x], xst, x, on_x)
    for i in range(2):
        arrive(f"zh{i}", raw.at[c, far, top[i]])
        for _, p in on_y.peers:
            start(f"far{i}", raw.at[c, far, top[i]], raw.at[c, far, top[i]], on_y(p))
    arrive("near", raw.at[c, pl.ds(0, 3)])
    start("sib0", raw.at[c, near4], raw.at[c, near4], sib)
    collect("xst", xst, on_x)
    yst[y] = (xst[0] + xst[1]) + (xst[2] + xst[3])
    spread("yst", lambda p: yst.at[y], yst, y, on_y)
    def far_rows():
        for i in range(2):
            arrive(f"far{i}", raw.at[c, pl.ds(0, 3), top[i]])
            start(f"sib{i + 1}", raw.at[c, far4, top[i]], raw.at[c, far4, top[i]], sib)
        for i in range(2):
            arrive(f"sib{i + 1}", raw.at[oc, far4, top[i]])

    def norm(i, carry):
        b = lax.rem(i + zh * 4, 8)
        tile = yst[lax.rem(b, 4)]
        stat = jnp.where(b < 4, tile[0:1, :], tile[4:5, :])

        def column(at):
            return jnp.sum(jnp.where(lane == row64 + at, stat, 0.0), axis=1, keepdims=True)

        average = column(0) / D
        variance = column(64) / D - average * average
        scale = lax.rsqrt(variance + EPS)
        rows = pl.ds(pl.multiple_of(b * 64, 64), 64)
        for k in range(2):
            block = (raw[k, b].astype(F32) - average) * scale * gains[k, 0:1, :]
            normed[rows, k * KP : k * KP + KB] = block.astype(BF16)
        return carry

    load_q.wait()
    load_kv.wait()
    arrive("wq", wq.at[mine])
    arrive("wkv", wkv.at[mine])
    for i in range(2):
        if i == 0:
            arrive("gain", gains.at[oc])
            collect("yst", yst, on_y)
            arrive("sib0", raw.at[oc, near4])
        else:
            far_rows()
        lax.fori_loop(4 * i, 4 * i + 4, norm, 0)
        side = zh if i == 0 else 1 - zh
        rows = normed[pl.ds(pl.multiple_of(side * 256, 256), 256), :]
        query = jnp.dot(rows, wq[...], preferred_element_type=F32)
        for zz in range(2):
            for xx in range(4):
                at = zz * 128 + xx * 32
                pq[xx, side * 2 + zz] = query[at : at + 32]
        two = pl.ds(side * 2, 2)
        for _, p in on_x.peers:
            start("qx", pq.at[p, two], rq.at[x, two], on_x(p))
    k64 = lax.broadcasted_iota(jnp.int32, (64, 512), 0)
    r512 = lax.broadcasted_iota(jnp.int32, (64, 512), 1)
    pick = r512 == (k64 >> 1) * 16 + n * 2 + (k64 & 1)
    chosen = jnp.dot(
        jnp.where(pick, 1.0, 0.0).astype(BF16), normed[...], preferred_element_type=F32
    ).astype(BF16)
    kvs[...] = jnp.dot(chosen, wkv[...], preferred_element_type=F32)
    for zz in range(4):
        for xx in range(4):
            at = zz * 16 + xx * 4
            kvp[xx, zz, 0:4, :] = kvs[at : at + 4, 0:128]
            kvp[xx, zz, 4:8, :] = kvs[at : at + 4, 128:256]
    spread("kx", lambda p: kvp.at[p], kvr, x, on_x)

    def part_q1():
        collect("qx", rq, on_x)
        total = pq[x]
        for _, p in on_x.peers:
            total = total + rq[p]
        for zz in range(4):
            for hh in range(2):
                to = hh * 4 + zz
                zq[to, 0:8] = total[zz, hh * 8 : hh * 8 + 8]
                zq[to, 8:16] = total[zz, 16 + hh * 8 : 24 + hh * 8]
        zqr[z] = zq[z]
        spread("qz", lambda p: zq.at[p], zqr, z, on_z)
        collect("kx", kvr, on_x)
        fresh = kvp[x]
        for _, p in on_x.peers:
            fresh = fresh + kvr[p]
        kz[...] = fresh
        spread("kz", lambda p: kz.at[p], kzr, zl, on_zl)

    def part_q2():
        collect("qz", zqr, on_z)
        sums = [(zqr[k] + zqr[k + 1]) + (zqr[k + 2] + zqr[k + 3]) for k in (0, 4)]
        for hh in range(2):
            cx[hh] = sums[hh]
        for cc in range(2):
            for yy in range(4):
                for hh in range(2):
                    at = cc * 8 + yy * 2
                    yt[cc, yy, hh * 2 : hh * 2 + 2, :] = cx[hh, at : at + 2, :]
        here = c * 4 + y
        yr[here] = yt[c, y]
        for _, p in on_y.peers:
            start("qy", yt.at[c, p], yr.at[here], on_y(p))
            start("qy", yt.at[oc, p], yr.at[here], on_y_sib(p))
        start("qy", yt.at[oc, y], yr.at[here], sib)
        collect("kz", kzr, on_zl)
        fresh = kz[zl]
        for _, p in zl_peers:
            fresh = fresh + kzr[p]
        kc[c] = fresh
        start("kc", kc.at[c], kc.at[c], sib)

    def part_q4():
        arrive("kc", kc.at[oc])
        arrive("qy", yr.at[pl.ds(0, 7)])
        for yy in range(4):
            at = yy * 4
            q48[at : at + 4, :] = yr[yy, 0:4, 0:256]
            q48[16 + at : 20 + at, 0:128] = yr[yy, 0:4, 256:384]
            q48[16 + at : 20 + at, 128:256] = yr[4 + yy, 0:4, 0:128]
            q48[32 + at : 36 + at, :] = yr[4 + yy, 0:4, 128:384]
        load_k.wait()
        load_v.wait()
        q = q48[...].astype(BF16)
        factor = 1.0 / 16.0
        first = lax.broadcasted_iota(jnp.int32, (48, 1), 0) % 2 == 0

        def fresh(k):
            tile = kc[k].astype(BF16).astype(F32)
            sides = []
            for at in (0, 4):
                pair = jnp.where(c == 0, tile[at : at + 2], tile[at + 2 : at + 4])
                sides.append(jnp.where(first, pair[0:1, :], pair[1:2, :]))
            return jnp.concatenate(sides, axis=1)

        def scores_of(r):
            return lax.dot_general(q, keys[r], (((1,), (1,)), ((), ())), preferred_element_type=F32)

        scores = jnp.where(first, scores_of(0), scores_of(1)) * factor
        own_score = jnp.sum(q.astype(F32) * fresh(0), axis=1, keepdims=True) * factor
        position = lax.broadcasted_iota(jnp.int32, (48, 384), 1)
        usable = position < jnp.where(first, lengths[0], lengths[1])
        masked = jnp.where(usable, scores, -1e30)
        highest = jnp.maximum(jnp.max(masked, axis=1, keepdims=True), own_score)
        exps = jnp.where(usable, jnp.exp(masked - highest), 0.0)
        own_exp = jnp.exp(own_score - highest)
        denominator = jnp.sum(exps, axis=1, keepdims=True) + own_exp
        weights = (exps / denominator).astype(BF16)
        own_weight = (own_exp / denominator).astype(BF16).astype(F32)

        def mixed(r):
            return jnp.dot(weights, values[r], preferred_element_type=F32)

        context = jnp.where(first, mixed(0), mixed(1)) + own_weight * fresh(1)
        ctx[...] = context
        for t in range(3):
            for yy in range(4):
                for hh in range(2):
                    at = t * 16 + yy * 4 + hh * 2
                    caf[hh, yy * 8 + t * 2 : yy * 8 + t * 2 + 2, :] = ctx[at : at + 2, :]
        ca[...] = caf[...].astype(BF16)
        ar[z] = ca[zh]
        spread("a", lambda p: ca.at[p // 4], ar, z, on_z)

    def part_c1():
        collect("a", ar, on_z)
        for yy in range(4):
            bs[yy] = ar[:, yy * 8 : yy * 8 + 8, :].astype(F32).reshape(64, 256).astype(BF16)
        br[y] = bs[y]
        spread("b", lambda p: bs.at[p], br, y, on_y)

    def part_c2():
        collect("b", br, on_y)
        brf[...] = br[...].astype(F32)
        for t in range(3):
            for zz in range(4):
                for hh in range(2):
                    for yy in range(4):
                        to = zz * 16 + hh * 8 + yy * 2
                        at = (hh * 4 + zz) * 8 + t * 2
                        ctf[to : to + 2, t * 256 : t * 256 + 256] = brf[yy, at : at + 2, :]
        ct[x] = ctf[...].astype(BF16)
        for _, p in on_x.peers:
            start("c", ct.at[x], ct.at[x], on_x(p))

    def part_c4():
        load_o.wait()
        arrive("wo", wo.at[oc])
        collect("c", ct, on_x)
        for cc in range(2):
            out = lax.dot_general(
                ct[...].reshape(256, 768),
                wo[cc],
                (((1,), (1,)), ((), ())),
                preferred_element_type=F32,
            )
            for xx in range(4):
                for zz in range(4):
                    at = xx * 64 + zz * 16
                    to = (xx % 2) * 16
                    i = jnp.where(zh == zz // 2, 1, 0)
                    block = out[at : at + 16].astype(BF16)
                    os_[i, (zz % 2) * 2 + xx // 2, cc, to : to + 16, :] = block
        for i in range(2):
            spread(f"e{i}", lambda p, i=i: os_.at[i, p], or_.at[i], y, on_y)

    def summed(i):
        collect(f"e{i}", or_.at[i], on_y)
        total = os_[i, y].astype(F32)
        for _, p in on_y.peers:
            total = total + or_[i, p].astype(F32)
        return total

    def part_c5():
        fs[...] = summed(0).astype(BF16)
        start("f", fs.at[c], fr.at[0], partner)
        start("f", fs.at[oc], fr.at[1], partner_sib)
        vf[...] = summed(1)
        gs[...] = vf[oc].astype(BF16)
        start("g", gs, gr, sib)

    right, left = lax.rem(x + 1, 4), lax.rem(x + 3, 4)
    across = lax.rem(x + 2, 4)

    def first_copies(j):
        for k, to in enumerate((right, left)):
            src = part.at[j, :, across, :, pl.ds(k * CW, CW)]
            remote(src, r1.at[j, k], chunk_1.at[0], chunk_1.at[1 + j], on_x(to)).start()

    def came(sems, j, dst):
        remote(dst, dst, sems.at[0], sems.at[1 + j], sib).wait_recv()

    def z_first(j):
        return functools.reduce(jnp.logical_or, [j == b for b in Z_FIRST])

    def z_index(j):
        return sum([jnp.where(j > b, 1, 0) for b in Z_FIRST[:-1]], 0)

    def multiply(j):
        def ready():
            three = pl.ds(j, 3)
            to = wgu.at[three, mine]
            local(to, to, 6 + j // 3).wait()
            remote(to, to, chunk_w.at[0], chunk_w.at[1 + j // 3], sib).wait_recv()

        pl.when(lax.rem(j, 3) == 0)(ready)
        product = jnp.dot(normed[...], wgu[j], preferred_element_type=F32)
        part[j] = product.astype(BF16).reshape(4, 4, 32, 2 * CW)

        @pl.when(jnp.logical_not(z_first(j)))
        def _():
            first_copies(j)

        @pl.when(z_first(j))
        def _():
            for _, p in zl_peers:
                to = zb.at[z_index(j), zl]
                remote(part.at[j, p], to, chunk_1.at[0], chunk_1.at[1 + j], on_zl(p)).start()

    def add_first(j):
        came(chunk_1, j, r1.at[j])
        for k, to in enumerate((right, left)):
            for m in range(2):
                cols = slice(m * CW, m * CW + CW)
                if m == k:
                    total = part[j, :, to, :, cols].astype(F32) + r1[j, k].astype(F32)
                    s1[j, k, :, :, cols] = total.astype(BF16)
                else:
                    s1[j, k, :, :, cols] = part[j, :, to, :, cols]
            remote(s1.at[j, k], r2.at[j, k], chunk_2.at[0], chunk_2.at[1 + j], on_x(to)).start()

    def add_second(j):
        came(chunk_2, j, r2.at[j])
        total = part[j, :, x].astype(F32) + r2[j, 0].astype(F32) + r2[j, 1].astype(F32)
        zs[j] = total.astype(BF16)
        for _, p in zl_peers:
            remote(zs.at[j, p], zr.at[j, zl], chunk_3.at[0], chunk_3.at[1 + j], on_zl(p)).start()

    def add_z(j):
        i = z_index(j)
        came(chunk_1, j, zb.at[i, pl.ds(0, 3)])
        total = part[j, zl].astype(F32)
        for _, p in zl_peers:
            total = total + zb[i, p].astype(F32)
        xs[i] = total.astype(BF16)
        for _, p in on_x.peers:
            remote(xs.at[i, p], xr.at[i, x], chunk_2.at[0], chunk_2.at[1 + j], on_x(p)).start()

    def gated(j, total):
        g = total[:, :CW]
        hidden_units = (g * (1.0 / (1.0 + jnp.exp(-g))) * total[:, CW:]).astype(BF16)
        sl[j] = hidden_units.reshape(2, 16, CW)
        start("last", sl.at[j, 1 - c], sr.at[j], sib)
        slab[:, pl.ds(pl.multiple_of(half + j * CW, 128), CW)] = sl[j, c]

    def finish(j):
        came(chunk_3, j, zr.at[j, pl.ds(0, 3)])
        total = zs[j, zl].astype(F32)
        for _, p in zl_peers:
            total = total + zr[j, p].astype(F32)
        gated(j, total)

    def finish_z(j):
        i = z_index(j)
        came(chunk_2, j, xr.at[i, pl.ds(0, 3)])
        total = xs[i, x].astype(F32)
        for _, p in on_x.peers:
            total = total + xr[i, p].astype(F32)
        gated(j, total)

    parts = dict(
        Q1=part_q1, Q2=part_q2, Q4=part_q4, C1=part_c1, C2=part_c2, C4=part_c4, C5=part_c5
    )

    def step(k, carry):
        for name, run in parts.items():
            pl.when(k == STEP[name])(run)
        for lag, run, z_kind in (
            (LAG3, finish, False),
            (Z_LAG2, finish_z, True),
            (LAG2, add_second, False),
            (Z_LAG1, add_z, True),
            (LAG1, add_first, False),
            (0, multiply, None),
        ):
            j = k - lag
            due = jnp.logical_and(j >= 0, j < CHUNKS)
            if z_kind is not None:
                due = jnp.logical_and(due, z_first(j) == z_kind)
            pl.when(due)(functools.partial(run, j))
        return carry

    lax.fori_loop(0, STEPS, step, 0)

    arrive("last", sr)

    def rest(j, carry):
        slab[:, pl.ds(pl.multiple_of(other + j * CW, 128), CW)] = sr[j]
        return carry

    lax.fori_loop(0, CHUNKS, rest, 0)
    arrive("f", fr)
    arrive("g", gr)
    for core, total in ((c, vf[c] + fr[0].astype(F32)), (oc, gr[...].astype(F32) + fr[1].astype(F32))):
        for xx in range(2):
            rows = pl.ds(pl.multiple_of(xx * 32 + core * 16, 16), 16)
            update[rows, :] = total[xx * 16 : xx * 16 + 16].astype(BF16)

    of3, of7 = pl.ds(0, 3), pl.ds(0, 7)
    left_bytes = dict(
        cst=cst.at[0], zst=zst.at[of7], xst=xst.at[of3], yst=yst.at[of3], gain=gains.at[0],
        near=raw.at[0, of3], zh0=raw.at[0, 0, top[0]], zh1=raw.at[0, 0, top[0]],
        far0=raw.at[0, of3, top[0]], far1=raw.at[0, of3, top[0]], sib0=raw.at[0, pl.ds(0, 4)],
        sib1=raw.at[0, pl.ds(0, 4), top[0]], sib2=raw.at[0, pl.ds(0, 4), top[0]], wq=wq.at[pl.ds(0, KB)], wkv=wkv.at[pl.ds(0, KB)],
        qx=rq.at[of3], kx=kvr.at[of3], qz=zqr.at[of7], kz=kzr.at[of3], kc=kc.at[0], wo=wo.at[0],
        qy=yr.at[of7], a=ar.at[of7], b=br.at[of3], c=ct.at[of3],
        e0=or_.at[0, of3], e1=or_.at[1, of3], f=fr, g=gr, last=sr,
    )
    for name, dst in left_bytes.items():
        remote(dst, dst, sent.at[slot[name]], come.at[slot[name]], sib).wait_send()

    def gone(sems, dst):
        remote(dst, dst, sems.at[0], sems.at[1], sib).wait_send()

    a_kind, b_kind = pl.ds(0, CHUNKS - len(Z_FIRST)), pl.ds(0, len(Z_FIRST))
    gone(chunk_w, wgu.at[:, mine])
    gone(chunk_1, r1.at[a_kind])
    gone(chunk_1, zb.at[:, pl.ds(0, 3)])
    gone(chunk_2, r2.at[a_kind])
    gone(chunk_2, xr.at[:, pl.ds(0, 3)])
    gone(chunk_3, zr.at[a_kind, pl.ds(0, 3)])


def scratch():
    v = pltpu.VMEM
    z_chunks = len(Z_FIRST)
    buffers = [
        v((2, 8, 64, KB), BF16),
        v((512, 2 * KP), BF16),
        v((2, 8, KB), F32),
        v((CHUNKS, 2 * KP, 2 * CW), BF16),
        v((2 * KP, 384), BF16),
        v((2 * KP, 256), BF16),
        v((2, KB, 768), BF16),
        v((2, 384, 256), BF16),
        v((2, 384, 256), BF16),
        v((2, 8, 128), F32),
        v((8, 8, 128), F32),
        v((4, 8, 128), F32),
        v((4, 8, 128), F32),
        v((CHUNKS, 4, 4, 32, 2 * CW), BF16),
        v((CHUNKS, 2, 4, 32, CW), BF16),
        v((CHUNKS, 2, 4, 32, 2 * CW), BF16),
        v((CHUNKS, 2, 4, 32, 2 * CW), BF16),
        v((CHUNKS, 4, 32, 2 * CW), BF16),
        v((CHUNKS, 4, 32, 2 * CW), BF16),
        v((z_chunks, 4, 4, 32, 2 * CW), BF16),
        v((z_chunks, 4, 32, 2 * CW), BF16),
        v((z_chunks, 4, 32, 2 * CW), BF16),
        v((CHUNKS, 2, 16, CW), BF16),
        v((CHUNKS, 16, CW), BF16),
        v((64, 256), F32),
        v((4, 4, 8, 128), F32),
        v((4, 4, 8, 128), F32),
        v((4, 8, 128), F32),
        v((4, 8, 128), F32),
        v((2, 8, 128), F32),
        v((4, 4, 32, 384), F32),
        v((4, 4, 32, 384), F32),
        v((8, 16, 384), F32),
        v((8, 16, 384), F32),
        v((2, 16, 384), F32),
        v((2, 4, 8, 384), F32),
        v((8, 8, 384), F32),
        v((48, 256), F32),
        v((48, 256), F32),
        v((2, 32, 256), F32),
        v((2, 32, 256), BF16),
        v((8, 32, 256), BF16),
        v((4, 64, 256), BF16),
        v((4, 64, 256), BF16),
        v((4, 64, 256), F32),
        v((64, 768), F32),
        v((4, 64, 768), BF16),
        v((2, 4, 2, 32, KB), BF16),
        v((2, 4, 2, 32, KB), BF16),
        v((2, 32, KB), F32),
        v((2, 32, KB), BF16),
        v((2, 32, KB), BF16),
        v((32, KB), BF16),
        v((32, KB), BF16),
    ]
    counts = (9, 30, 30, 4, 1 + CHUNKS, 1 + CHUNKS, 1 + CHUNKS)
    return buffers + [pltpu.SemaphoreType.DMA((count,)) for count in counts]


def copy_out(update, slab, update_out, slab_out):
    update_out[...] = update[...]
    slab_out[...] = slab[...]


def local(hidden, gain, gate_w, up_w, query_w, kv_w, out_w, *rest):
    anywhere = pl.BlockSpec(memory_space=pl.ANY)
    vmem = pl.BlockSpec(memory_space=pltpu.VMEM)
    shapes = (
        jax.ShapeDtypeStruct((64, KB), BF16),
        jax.ShapeDtypeStruct((16, 2 * HALF), BF16),
    )
    results = pl.pallas_call(
        kernel,
        out_shape=shapes,
        in_specs=[anywhere, vmem] + [anywhere] * 7 + [pl.BlockSpec(memory_space=pltpu.SMEM)],
        out_specs=(vmem, vmem),
        scratch_shapes=scratch(),
        compiler_params=pltpu.CompilerParams(
            collective_id=0, has_side_effects=True, vmem_limit_bytes=58 * 1024 * 1024
        ),
        name="layer",
    )(hidden, gain, gate_w, up_w, query_w, kv_w, out_w.T, *rest)
    return pl.pallas_call(
        copy_out,
        out_shape=shapes,
        in_specs=[vmem, vmem],
        out_specs=(vmem, vmem),
        name="outputs",
    )(*results)


def solution(mesh):
    placed = (
        P("narrow", "wide"),
        P("wide"),
        P("wide", "narrow"),
        P("wide", "narrow"),
        P("wide", "narrow"),
        P("wide", None),
        P("narrow", "wide"),
        P(("wide", "narrow"), None, None),
        P(("wide", "narrow"), None, None),
        P(("wide", "narrow")),
    )
    return jax.shard_map(
        local,
        mesh=mesh,
        in_specs=placed,
        out_specs=(P("narrow", "wide"), P("wide", "narrow")),
        check_vma=False,
    )
```

```python
import functools

import jax
import jax.numpy as jnp
from jax import lax
from jax.experimental import pallas as pl
from jax.experimental.pallas import tpu as pltpu
from jax.sharding import PartitionSpec as P

D = 18432
EPS = 1e-05
MESH = pl.DeviceIdType.MESH
F32 = jnp.float32
BF16 = jnp.bfloat16
KB = 576
KP = 640
CHUNKS = 9
CW = 256
HALF = CHUNKS * CW

STEP = dict(Q1=2, Q2=5, Q4=7, C1=8, C2=9, C4=11, C5=13)
LAG1, LAG2, LAG3 = 2, 4, 6
Z_LAG1, Z_LAG2 = 4, 7
Z_FIRST = (0,)
STEPS = 16


def device(x, y, zl, zh, c):
    return ((zl * 4 + x) * 2 + c, zh * 4 + y)


def kernel(
    hidden,
    gain,
    gate_w,
    up_w,
    query_w,
    kv_w,
    out_w,
    keys_h,
    values_h,
    lengths,
    update,
    slab,
    raw,
    normed,
    gains,
    wgu,
    wq,
    wkv,
    wo,
    keys,
    values,
    cst,
    zst,
    xst,
    yst,
    part,
    r1,
    s1,
    r2,
    zs,
    zr,
    zb,
    xs,
    xr,
    sl,
    sr,
    kvs,
    kvp,
    kvr,
    kz,
    kzr,
    kc,
    pq,
    rq,
    zq,
    zqr,
    cx,
    yt,
    yr,
    q48,
    ctx,
    caf,
    ca,
    ar,
    bs,
    br,
    brf,
    ctf,
    ct,
    os_,
    or_,
    vf,
    fs,
    fr,
    gs,
    gr,
    lsem,
    sent,
    come,
    chunk_w,
    chunk_1,
    chunk_2,
    chunk_3,
):
    w = lax.axis_index("wide")
    n = lax.axis_index("narrow")
    c = lax.rem(w, 2)
    x = lax.rem(w // 2, 4)
    zl = w // 8
    zh = n // 4
    y = lax.rem(n, 4)
    z = zh * 4 + zl
    oc = 1 - c
    sib = device(x, y, zl, zh, 1 - c)
    partner = device(x, y, zl, 1 - zh, c)
    partner_sib = device(x, y, zl, 1 - zh, oc)

    def on_x(p):
        return device(p, y, zl, zh, c)

    def on_y(p):
        return device(x, p, zl, zh, c)

    def on_y_sib(p):
        return device(x, p, zl, zh, oc)

    def on_z(p):
        return device(x, y, lax.rem(p, 4), p // 4, c)

    def remote(src, dst, ss, rs, to):
        return pltpu.make_async_remote_copy(
            src_ref=src, dst_ref=dst, send_sem=ss, recv_sem=rs, device_id=to, device_id_type=MESH
        )

    def peers(me, size):
        return [(d, lax.rem(me + d, size)) for d in range(1, size)]

    on_x.peers, on_y.peers, on_z.peers = peers(x, 4), peers(y, 4), peers(z, 8)
    zl_peers = peers(zl, 4)

    def on_zl(p):
        return device(x, y, p, zh, c)

    on_zl.peers = zl_peers

    names = (
        "cst", "zst", "xst", "yst", "gain", "near", "zh0", "zh1", "far0", "far1", "sib0", "sib1", "sib2", "wq", "wkv",
        "wo", "qx", "kx", "qz", "kz", "kc", "qy", "a", "b", "c", "e0", "e1", "f", "g",
        "last",
    )
    slot = {name: i for i, name in enumerate(names)}

    def start(name, src, dst, to):
        remote(src, dst, sent.at[slot[name]], come.at[slot[name]], to).start()

    def arrive(name, dst):
        remote(dst, dst, sent.at[slot[name]], come.at[slot[name]], sib).wait_recv()

    def spread(name, src, dst, me, on):
        for _, p in on.peers:
            start(name, src(p), dst.at[me], on(p))

    def collect(name, dst, on):
        arrive(name, dst.at[pl.ds(0, len(on.peers))])

    half = pl.multiple_of(c * HALF, 128)
    other = pl.multiple_of((1 - c) * HALF, 128)
    mine = pl.ds(pl.multiple_of(c * KP, 128), KB)

    def local(src, dst, i):
        return pltpu.make_async_copy(src, dst, lsem.at[i])

    load_x = local(hidden, raw.at[c, n], 0)
    load_x.start()
    load_q = local(query_w.at[:, pl.ds(pl.multiple_of(c * 384, 128), 384)], wq.at[mine], 1)
    load_kv = local(kv_w.at[:, pl.ds(pl.multiple_of(c * 256, 128), 256)], wkv.at[mine], 2)
    load_o = local(out_w, wo.at[c], 3)
    load_k = local(keys_h, keys, 4)
    load_v = local(values_h, values, 5)
    load_q.start()
    load_kv.start()

    barrier = pltpu.get_barrier_semaphore()
    greeted = [on(p) for on in (on_z, on_x, on_y) for _, p in on.peers] + [sib]
    greeted += [on_y_sib(p) for _, p in on_y.peers] + [partner_sib]
    for to in greeted:
        pl.semaphore_signal(barrier, inc=1, device_id=to, device_id_type=MESH)

    for k in range(2):
        pad = pl.ds(k * KP + KB, KP - KB)
        normed[:, pad] = jnp.zeros((512, KP - KB), BF16)
        wq[pad, :] = jnp.zeros((KP - KB, 384), BF16)
        wkv[pad, :] = jnp.zeros((KP - KB, 256), BF16)

        def fill(j, carry, pad=pad):
            wgu[j, pad, :] = jnp.zeros((KP - KB, 2 * CW), BF16)
            return carry

        lax.fori_loop(0, CHUNKS, fill, 0)
    caf[...] = jnp.zeros((2, 32, 256), F32)
    yt[...] = jnp.zeros((2, 4, 8, 384), F32)
    load_x.wait()
    own = raw[c, n].astype(F32)
    row64 = lax.broadcasted_iota(jnp.int32, (64, 128), 0)
    lane = lax.broadcasted_iota(jnp.int32, (64, 128), 1)
    both = jnp.where(
        lane < 64,
        jnp.sum(own, axis=1, keepdims=True),
        jnp.sum(own * own, axis=1, keepdims=True),
    )
    line = jnp.sum(jnp.where((lane & 63) == row64, both, 0.0), axis=0, keepdims=True)
    cst[c] = jnp.broadcast_to(line, (8, 128))
    gains[c] = jnp.broadcast_to(gain[...].reshape(1, KB), (8, KB))

    pl.semaphore_wait(barrier, len(greeted))

    start("cst", cst.at[c], cst.at[c], sib)
    top = [pl.ds(0, 32), pl.ds(32, 32)]
    for i in range(2):
        start(f"zh{i}", raw.at[c, n, top[i]], raw.at[c, n, top[i]], partner)
    for _, p in on_y.peers:
        start("near", raw.at[c, n], raw.at[c, n], on_y(p))
    start("gain", gains.at[c], gains.at[c], sib)
    arrive("cst", cst.at[oc])
    zst[z] = cst[0] + cst[1]
    spread("zst", lambda p: zst.at[z], zst, z, on_z)
    away_q = pl.ds(pl.multiple_of((1 - c) * 384, 128), 384)
    away_kv = pl.ds(pl.multiple_of((1 - c) * 256, 128), 256)
    start("wq", query_w.at[:, away_q], wq.at[mine], sib)
    start("wkv", kv_w.at[:, away_kv], wkv.at[mine], sib)

    def start_weights(j, carry):
        g = j // 3
        for k, weight in enumerate((gate_w, up_w)):
            to = wgu.at[j, mine, pl.ds(k * CW, CW)]
            there = weight.at[:, pl.ds(pl.multiple_of(other + j * CW, 128), CW)]
            remote(there, to, chunk_w.at[0], chunk_w.at[1 + g], sib).start()
            here = weight.at[:, pl.ds(pl.multiple_of(half + j * CW, 128), CW)]
            local(here, to, 6 + g).start()
        return carry

    lax.fori_loop(0, CHUNKS, start_weights, 0)
    start("wo", out_w, wo.at[c], sib)
    load_o.start()
    load_k.start()
    load_v.start()

    far = (1 - zh) * 4 + y
    near4 = pl.ds(zh * 4, 4)
    far4 = pl.ds((1 - zh) * 4, 4)
    collect("zst", zst, on_z)
    upper = lax.broadcasted_iota(jnp.int32, (8, 128), 0) < 4
    xst[x] = jnp.where(
        upper, (zst[0] + zst[1]) + (zst[2] + zst[3]), (zst[4] + zst[5]) + (zst[6] + zst[7])
    )
    spread("xst", lambda p: xst.at[x], xst, x, on_x)
    for i in range(2):
        arrive(f"zh{i}", raw.at[c, far, top[i]])
        for _, p in on_y.peers:
            start(f"far{i}", raw.at[c, far, top[i]], raw.at[c, far, top[i]], on_y(p))
    arrive("near", raw.at[c, pl.ds(0, 3)])
    start("sib0", raw.at[c, near4], raw.at[c, near4], sib)
    collect("xst", xst, on_x)
    yst[y] = (xst[0] + xst[1]) + (xst[2] + xst[3])
    spread("yst", lambda p: yst.at[y], yst, y, on_y)
    def far_rows():
        for i in range(2):
            arrive(f"far{i}", raw.at[c, pl.ds(0, 3), top[i]])
            start(f"sib{i + 1}", raw.at[c, far4, top[i]], raw.at[c, far4, top[i]], sib)
        for i in range(2):
            arrive(f"sib{i + 1}", raw.at[oc, far4, top[i]])

    def norm(i, carry):
        b = lax.rem(i + zh * 4, 8)
        tile = yst[lax.rem(b, 4)]
        stat = jnp.where(b < 4, tile[0:1, :], tile[4:5, :])

        def column(at):
            return jnp.sum(jnp.where(lane == row64 + at, stat, 0.0), axis=1, keepdims=True)

        average = column(0) / D
        variance = column(64) / D - average * average
        scale = lax.rsqrt(variance + EPS)
        rows = pl.ds(pl.multiple_of(b * 64, 64), 64)
        for k in range(2):
            block = (raw[k, b].astype(F32) - average) * scale * gains[k, 0:1, :]
            normed[rows, k * KP : k * KP + KB] = block.astype(BF16)
        return carry

    load_q.wait()
    load_kv.wait()
    arrive("wq", wq.at[mine])
    arrive("wkv", wkv.at[mine])
    for i in range(2):
        if i == 0:
            arrive("gain", gains.at[oc])
            collect("yst", yst, on_y)
            arrive("sib0", raw.at[oc, near4])
        else:
            far_rows()
        lax.fori_loop(4 * i, 4 * i + 4, norm, 0)
        side = zh if i == 0 else 1 - zh
        rows = normed[pl.ds(pl.multiple_of(side * 256, 256), 256), :]
        query = jnp.dot(rows, wq[...], preferred_element_type=F32)
        for zz in range(2):
            for xx in range(4):
                at = zz * 128 + xx * 32
                pq[xx, side * 2 + zz] = query[at : at + 32]
        two = pl.ds(side * 2, 2)
        for _, p in on_x.peers:
            start("qx", pq.at[p, two], rq.at[x, two], on_x(p))
    k64 = lax.broadcasted_iota(jnp.int32, (64, 512), 0)
    r512 = lax.broadcasted_iota(jnp.int32, (64, 512), 1)
    pick = r512 == (k64 >> 1) * 16 + n * 2 + (k64 & 1)
    chosen = jnp.dot(
        jnp.where(pick, 1.0, 0.0).astype(BF16), normed[...], preferred_element_type=F32
    ).astype(BF16)
    kvs[...] = jnp.dot(chosen, wkv[...], preferred_element_type=F32)
    for zz in range(4):
        for xx in range(4):
            at = zz * 16 + xx * 4
            kvp[xx, zz, 0:4, :] = kvs[at : at + 4, 0:128]
            kvp[xx, zz, 4:8, :] = kvs[at : at + 4, 128:256]
    spread("kx", lambda p: kvp.at[p], kvr, x, on_x)

    def part_q1():
        collect("qx", rq, on_x)
        total = pq[x]
        for _, p in on_x.peers:
            total = total + rq[p]
        for zz in range(4):
            for hh in range(2):
                to = hh * 4 + zz
                zq[to, 0:8] = total[zz, hh * 8 : hh * 8 + 8]
                zq[to, 8:16] = total[zz, 16 + hh * 8 : 24 + hh * 8]
        zqr[z] = zq[z]
        spread("qz", lambda p: zq.at[p], zqr, z, on_z)
        collect("kx", kvr, on_x)
        fresh = kvp[x]
        for _, p in on_x.peers:
            fresh = fresh + kvr[p]
        kz[...] = fresh
        spread("kz", lambda p: kz.at[p], kzr, zl, on_zl)

    def part_q2():
        collect("qz", zqr, on_z)
        sums = [(zqr[k] + zqr[k + 1]) + (zqr[k + 2] + zqr[k + 3]) for k in (0, 4)]
        for hh in range(2):
            cx[hh] = sums[hh]
        for cc in range(2):
            for yy in range(4):
                for hh in range(2):
                    at = cc * 8 + yy * 2
                    yt[cc, yy, hh * 2 : hh * 2 + 2, :] = cx[hh, at : at + 2, :]
        here = c * 4 + y
        yr[here] = yt[c, y]
        for _, p in on_y.peers:
            start("qy", yt.at[c, p], yr.at[here], on_y(p))
            start("qy", yt.at[oc, p], yr.at[here], on_y_sib(p))
        start("qy", yt.at[oc, y], yr.at[here], sib)
        collect("kz", kzr, on_zl)
        fresh = kz[zl]
        for _, p in zl_peers:
            fresh = fresh + kzr[p]
        kc[c] = fresh
        start("kc", kc.at[c], kc.at[c], sib)

    def part_q4():
        arrive("kc", kc.at[oc])
        arrive("qy", yr.at[pl.ds(0, 7)])
        for yy in range(4):
            at = yy * 4
            q48[at : at + 4, :] = yr[yy, 0:4, 0:256]
            q48[16 + at : 20 + at, 0:128] = yr[yy, 0:4, 256:384]
            q48[16 + at : 20 + at, 128:256] = yr[4 + yy, 0:4, 0:128]
            q48[32 + at : 36 + at, :] = yr[4 + yy, 0:4, 128:384]
        load_k.wait()
        load_v.wait()
        q = q48[...].astype(BF16)
        factor = 1.0 / 16.0
        first = lax.broadcasted_iota(jnp.int32, (48, 1), 0) % 2 == 0

        def fresh(k):
            tile = kc[k].astype(BF16).astype(F32)
            sides = []
            for at in (0, 4):
                pair = jnp.where(c == 0, tile[at : at + 2], tile[at + 2 : at + 4])
                sides.append(jnp.where(first, pair[0:1, :], pair[1:2, :]))
            return jnp.concatenate(sides, axis=1)

        def scores_of(r):
            return lax.dot_general(q, keys[r], (((1,), (1,)), ((), ())), preferred_element_type=F32)

        scores = jnp.where(first, scores_of(0), scores_of(1)) * factor
        own_score = jnp.sum(q.astype(F32) * fresh(0), axis=1, keepdims=True) * factor
        position = lax.broadcasted_iota(jnp.int32, (48, 384), 1)
        usable = position < jnp.where(first, lengths[0], lengths[1])
        masked = jnp.where(usable, scores, -1e30)
        highest = jnp.maximum(jnp.max(masked, axis=1, keepdims=True), own_score)
        exps = jnp.where(usable, jnp.exp(masked - highest), 0.0)
        own_exp = jnp.exp(own_score - highest)
        denominator = jnp.sum(exps, axis=1, keepdims=True) + own_exp
        weights = (exps / denominator).astype(BF16)
        own_weight = (own_exp / denominator).astype(BF16).astype(F32)

        def mixed(r):
            return jnp.dot(weights, values[r], preferred_element_type=F32)

        context = jnp.where(first, mixed(0), mixed(1)) + own_weight * fresh(1)
        ctx[...] = context
        for t in range(3):
            for yy in range(4):
                for hh in range(2):
                    at = t * 16 + yy * 4 + hh * 2
                    caf[hh, yy * 8 + t * 2 : yy * 8 + t * 2 + 2, :] = ctx[at : at + 2, :]
        ca[...] = caf[...].astype(BF16)
        ar[z] = ca[zh]
        spread("a", lambda p: ca.at[p // 4], ar, z, on_z)

    def part_c1():
        collect("a", ar, on_z)
        for yy in range(4):
            bs[yy] = ar[:, yy * 8 : yy * 8 + 8, :].astype(F32).reshape(64, 256).astype(BF16)
        br[y] = bs[y]
        spread("b", lambda p: bs.at[p], br, y, on_y)

    def part_c2():
        collect("b", br, on_y)
        brf[...] = br[...].astype(F32)
        for t in range(3):
            for zz in range(4):
                for hh in range(2):
                    for yy in range(4):
                        to = zz * 16 + hh * 8 + yy * 2
                        at = (hh * 4 + zz) * 8 + t * 2
                        ctf[to : to + 2, t * 256 : t * 256 + 256] = brf[yy, at : at + 2, :]
        ct[x] = ctf[...].astype(BF16)
        for _, p in on_x.peers:
            start("c", ct.at[x], ct.at[x], on_x(p))

    def part_c4():
        load_o.wait()
        arrive("wo", wo.at[oc])
        collect("c", ct, on_x)
        for cc in range(2):
            out = lax.dot_general(
                ct[...].reshape(256, 768),
                wo[cc],
                (((1,), (1,)), ((), ())),
                preferred_element_type=F32,
            )
            for xx in range(4):
                for zz in range(4):
                    at = xx * 64 + zz * 16
                    to = (xx % 2) * 16
                    i = jnp.where(zh == zz // 2, 1, 0)
                    block = out[at : at + 16].astype(BF16)
                    os_[i, (zz % 2) * 2 + xx // 2, cc, to : to + 16, :] = block
        for i in range(2):
            spread(f"e{i}", lambda p, i=i: os_.at[i, p], or_.at[i], y, on_y)

    def summed(i):
        collect(f"e{i}", or_.at[i], on_y)
        total = os_[i, y].astype(F32)
        for _, p in on_y.peers:
            total = total + or_[i, p].astype(F32)
        return total

    def part_c5():
        fs[...] = summed(0).astype(BF16)
        start("f", fs.at[c], fr.at[0], partner)
        start("f", fs.at[oc], fr.at[1], partner_sib)
        vf[...] = summed(1)
        gs[...] = vf[oc].astype(BF16)
        start("g", gs, gr, sib)

    right, left = lax.rem(x + 1, 4), lax.rem(x + 3, 4)
    across = lax.rem(x + 2, 4)

    def first_copies(j):
        for k, to in enumerate((right, left)):
            src = part.at[j, :, across, :, pl.ds(k * CW, CW)]
            remote(src, r1.at[j, k], chunk_1.at[0], chunk_1.at[1 + j], on_x(to)).start()

    def came(sems, j, dst):
        remote(dst, dst, sems.at[0], sems.at[1 + j], sib).wait_recv()

    def z_first(j):
        return functools.reduce(jnp.logical_or, [j == b for b in Z_FIRST])

    def z_index(j):
        return sum([jnp.where(j > b, 1, 0) for b in Z_FIRST[:-1]], 0)

    def multiply(j):
        def ready():
            three = pl.ds(j, 3)
            to = wgu.at[three, mine]
            local(to, to, 6 + j // 3).wait()
            remote(to, to, chunk_w.at[0], chunk_w.at[1 + j // 3], sib).wait_recv()

        pl.when(lax.rem(j, 3) == 0)(ready)
        product = jnp.dot(normed[...], wgu[j], preferred_element_type=F32)
        part[j] = product.astype(BF16).reshape(4, 4, 32, 2 * CW)

        @pl.when(jnp.logical_not(z_first(j)))
        def _():
            first_copies(j)

        @pl.when(z_first(j))
        def _():
            for _, p in zl_peers:
                to = zb.at[z_index(j), zl]
                remote(part.at[j, p], to, chunk_1.at[0], chunk_1.at[1 + j], on_zl(p)).start()

    def add_first(j):
        came(chunk_1, j, r1.at[j])
        for k, to in enumerate((right, left)):
            for m in range(2):
                cols = slice(m * CW, m * CW + CW)
                if m == k:
                    total = part[j, :, to, :, cols].astype(F32) + r1[j, k].astype(F32)
                    s1[j, k, :, :, cols] = total.astype(BF16)
                else:
                    s1[j, k, :, :, cols] = part[j, :, to, :, cols]
            remote(s1.at[j, k], r2.at[j, k], chunk_2.at[0], chunk_2.at[1 + j], on_x(to)).start()

    def add_second(j):
        came(chunk_2, j, r2.at[j])
        total = part[j, :, x].astype(F32) + r2[j, 0].astype(F32) + r2[j, 1].astype(F32)
        zs[j] = total.astype(BF16)
        for _, p in zl_peers:
            remote(zs.at[j, p], zr.at[j, zl], chunk_3.at[0], chunk_3.at[1 + j], on_zl(p)).start()

    def add_z(j):
        i = z_index(j)
        came(chunk_1, j, zb.at[i, pl.ds(0, 3)])
        total = part[j, zl].astype(F32)
        for _, p in zl_peers:
            total = total + zb[i, p].astype(F32)
        xs[i] = total.astype(BF16)
        for _, p in on_x.peers:
            remote(xs.at[i, p], xr.at[i, x], chunk_2.at[0], chunk_2.at[1 + j], on_x(p)).start()

    def gated(j, total):
        g = total[:, :CW]
        hidden_units = (g * (1.0 / (1.0 + jnp.exp(-g))) * total[:, CW:]).astype(BF16)
        sl[j] = hidden_units.reshape(2, 16, CW)
        start("last", sl.at[j, 1 - c], sr.at[j], sib)
        slab[:, pl.ds(pl.multiple_of(half + j * CW, 128), CW)] = sl[j, c]

    def finish(j):
        came(chunk_3, j, zr.at[j, pl.ds(0, 3)])
        total = zs[j, zl].astype(F32)
        for _, p in zl_peers:
            total = total + zr[j, p].astype(F32)
        gated(j, total)

    def finish_z(j):
        i = z_index(j)
        came(chunk_2, j, xr.at[i, pl.ds(0, 3)])
        total = xs[i, x].astype(F32)
        for _, p in on_x.peers:
            total = total + xr[i, p].astype(F32)
        gated(j, total)

    parts = dict(
        Q1=part_q1, Q2=part_q2, Q4=part_q4, C1=part_c1, C2=part_c2, C4=part_c4, C5=part_c5
    )

    def step(k, carry):
        for name, run in parts.items():
            pl.when(k == STEP[name])(run)
        for lag, run, z_kind in (
            (0, multiply, None),
            (LAG1, add_first, False),
            (LAG3, finish, False),
            (Z_LAG2, finish_z, True),
            (LAG2, add_second, False),
            (Z_LAG1, add_z, True),
        ):
            j = k - lag
            due = jnp.logical_and(j >= 0, j < CHUNKS)
            if z_kind is not None:
                due = jnp.logical_and(due, z_first(j) == z_kind)
            pl.when(due)(functools.partial(run, j))
        return carry

    lax.fori_loop(0, STEPS, step, 0)

    arrive("last", sr)

    def rest(j, carry):
        slab[:, pl.ds(pl.multiple_of(other + j * CW, 128), CW)] = sr[j]
        return carry

    lax.fori_loop(0, CHUNKS, rest, 0)
    arrive("f", fr)
    arrive("g", gr)
    for core, total in ((c, vf[c] + fr[0].astype(F32)), (oc, gr[...].astype(F32) + fr[1].astype(F32))):
        for xx in range(2):
            rows = pl.ds(pl.multiple_of(xx * 32 + core * 16, 16), 16)
            update[rows, :] = total[xx * 16 : xx * 16 + 16].astype(BF16)

    of3, of7 = pl.ds(0, 3), pl.ds(0, 7)
    left_bytes = dict(
        cst=cst.at[0], zst=zst.at[of7], xst=xst.at[of3], yst=yst.at[of3], gain=gains.at[0],
        near=raw.at[0, of3], zh0=raw.at[0, 0, top[0]], zh1=raw.at[0, 0, top[0]],
        far0=raw.at[0, of3, top[0]], far1=raw.at[0, of3, top[0]], sib0=raw.at[0, pl.ds(0, 4)],
        sib1=raw.at[0, pl.ds(0, 4), top[0]], sib2=raw.at[0, pl.ds(0, 4), top[0]], wq=wq.at[pl.ds(0, KB)], wkv=wkv.at[pl.ds(0, KB)],
        qx=rq.at[of3], kx=kvr.at[of3], qz=zqr.at[of7], kz=kzr.at[of3], kc=kc.at[0], wo=wo.at[0],
        qy=yr.at[of7], a=ar.at[of7], b=br.at[of3], c=ct.at[of3],
        e0=or_.at[0, of3], e1=or_.at[1, of3], f=fr, g=gr, last=sr,
    )
    for name, dst in left_bytes.items():
        remote(dst, dst, sent.at[slot[name]], come.at[slot[name]], sib).wait_send()

    def gone(sems, dst):
        remote(dst, dst, sems.at[0], sems.at[1], sib).wait_send()

    a_kind, b_kind = pl.ds(0, CHUNKS - len(Z_FIRST)), pl.ds(0, len(Z_FIRST))
    gone(chunk_w, wgu.at[:, mine])
    gone(chunk_1, r1.at[a_kind])
    gone(chunk_1, zb.at[:, pl.ds(0, 3)])
    gone(chunk_2, r2.at[a_kind])
    gone(chunk_2, xr.at[:, pl.ds(0, 3)])
    gone(chunk_3, zr.at[a_kind, pl.ds(0, 3)])


def scratch():
    v = pltpu.VMEM
    z_chunks = len(Z_FIRST)
    buffers = [
        v((2, 8, 64, KB), BF16),
        v((512, 2 * KP), BF16),
        v((2, 8, KB), F32),
        v((CHUNKS, 2 * KP, 2 * CW), BF16),
        v((2 * KP, 384), BF16),
        v((2 * KP, 256), BF16),
        v((2, KB, 768), BF16),
        v((2, 384, 256), BF16),
        v((2, 384, 256), BF16),
        v((2, 8, 128), F32),
        v((8, 8, 128), F32),
        v((4, 8, 128), F32),
        v((4, 8, 128), F32),
        v((CHUNKS, 4, 4, 32, 2 * CW), BF16),
        v((CHUNKS, 2, 4, 32, CW), BF16),
        v((CHUNKS, 2, 4, 32, 2 * CW), BF16),
        v((CHUNKS, 2, 4, 32, 2 * CW), BF16),
        v((CHUNKS, 4, 32, 2 * CW), BF16),
        v((CHUNKS, 4, 32, 2 * CW), BF16),
        v((z_chunks, 4, 4, 32, 2 * CW), BF16),
        v((z_chunks, 4, 32, 2 * CW), BF16),
        v((z_chunks, 4, 32, 2 * CW), BF16),
        v((CHUNKS, 2, 16, CW), BF16),
        v((CHUNKS, 16, CW), BF16),
        v((64, 256), F32),
        v((4, 4, 8, 128), F32),
        v((4, 4, 8, 128), F32),
        v((4, 8, 128), F32),
        v((4, 8, 128), F32),
        v((2, 8, 128), F32),
        v((4, 4, 32, 384), F32),
        v((4, 4, 32, 384), F32),
        v((8, 16, 384), F32),
        v((8, 16, 384), F32),
        v((2, 16, 384), F32),
        v((2, 4, 8, 384), F32),
        v((8, 8, 384), F32),
        v((48, 256), F32),
        v((48, 256), F32),
        v((2, 32, 256), F32),
        v((2, 32, 256), BF16),
        v((8, 32, 256), BF16),
        v((4, 64, 256), BF16),
        v((4, 64, 256), BF16),
        v((4, 64, 256), F32),
        v((64, 768), F32),
        v((4, 64, 768), BF16),
        v((2, 4, 2, 32, KB), BF16),
        v((2, 4, 2, 32, KB), BF16),
        v((2, 32, KB), F32),
        v((2, 32, KB), BF16),
        v((2, 32, KB), BF16),
        v((32, KB), BF16),
        v((32, KB), BF16),
    ]
    counts = (9, 30, 30, 4, 1 + CHUNKS, 1 + CHUNKS, 1 + CHUNKS)
    return buffers + [pltpu.SemaphoreType.DMA((count,)) for count in counts]


def copy_out(update, slab, update_out, slab_out):
    update_out[...] = update[...]
    slab_out[...] = slab[...]


def local(hidden, gain, gate_w, up_w, query_w, kv_w, out_w, *rest):
    anywhere = pl.BlockSpec(memory_space=pl.ANY)
    vmem = pl.BlockSpec(memory_space=pltpu.VMEM)
    shapes = (
        jax.ShapeDtypeStruct((64, KB), BF16),
        jax.ShapeDtypeStruct((16, 2 * HALF), BF16),
    )
    results = pl.pallas_call(
        kernel,
        out_shape=shapes,
        in_specs=[anywhere, vmem] + [anywhere] * 7 + [pl.BlockSpec(memory_space=pltpu.SMEM)],
        out_specs=(vmem, vmem),
        scratch_shapes=scratch(),
        compiler_params=pltpu.CompilerParams(
            collective_id=0, has_side_effects=True, vmem_limit_bytes=58 * 1024 * 1024
        ),
        name="layer",
    )(hidden, gain, gate_w, up_w, query_w, kv_w, out_w.T, *rest)
    return pl.pallas_call(
        copy_out,
        out_shape=shapes,
        in_specs=[vmem, vmem],
        out_specs=(vmem, vmem),
        name="outputs",
    )(*results)


def solution(mesh):
    placed = (
        P("narrow", "wide"),
        P("wide"),
        P("wide", "narrow"),
        P("wide", "narrow"),
        P("wide", "narrow"),
        P("wide", None),
        P("narrow", "wide"),
        P(("wide", "narrow"), None, None),
        P(("wide", "narrow"), None, None),
        P(("wide", "narrow")),
    )
    return jax.shard_map(
        local,
        mesh=mesh,
        in_specs=placed,
        out_specs=(P("narrow", "wide"), P("wide", "narrow")),
        check_vma=False,
    )
```

```python
import functools

import jax
import jax.numpy as jnp
from jax import lax
from jax.experimental import pallas as pl
from jax.experimental.pallas import tpu as pltpu
from jax.sharding import PartitionSpec as P

D = 18432
EPS = 1e-05
MESH = pl.DeviceIdType.MESH
F32 = jnp.float32
BF16 = jnp.bfloat16
KB = 576
KP = 640
CHUNKS = 9
CW = 256
HALF = CHUNKS * CW

STEP = dict(Q1=2, Q2=5, Q4=7, C1=8, C2=9, C4=11, C5=13)
LAG1, LAG2, LAG3 = 2, 4, 7
Z_LAG1, Z_LAG2 = 4, 7
Z_FIRST = (0,)
STEPS = 16


def device(x, y, zl, zh, c):
    return ((zl * 4 + x) * 2 + c, zh * 4 + y)


def kernel(
    hidden,
    gain,
    gate_w,
    up_w,
    query_w,
    kv_w,
    out_w,
    keys_h,
    values_h,
    lengths,
    update,
    slab,
    raw,
    normed,
    gains,
    wgu,
    wq,
    wkv,
    wo,
    keys,
    values,
    cst,
    zst,
    xst,
    yst,
    part,
    r1,
    s1,
    r2,
    zs,
    zr,
    zb,
    xs,
    xr,
    sl,
    sr,
    kvs,
    kvp,
    kvr,
    kz,
    kzr,
    kc,
    pq,
    rq,
    zq,
    zqr,
    cx,
    yt,
    yr,
    q48,
    ctx,
    caf,
    ca,
    ar,
    bs,
    br,
    brf,
    ctf,
    ct,
    os_,
    or_,
    vf,
    fs,
    fr,
    gs,
    gr,
    lsem,
    sent,
    come,
    chunk_w,
    chunk_1,
    chunk_2,
    chunk_3,
):
    w = lax.axis_index("wide")
    n = lax.axis_index("narrow")
    c = lax.rem(w, 2)
    x = lax.rem(w // 2, 4)
    zl = w // 8
    zh = n // 4
    y = lax.rem(n, 4)
    z = zh * 4 + zl
    oc = 1 - c
    sib = device(x, y, zl, zh, 1 - c)
    partner = device(x, y, zl, 1 - zh, c)
    partner_sib = device(x, y, zl, 1 - zh, oc)

    def on_x(p):
        return device(p, y, zl, zh, c)

    def on_y(p):
        return device(x, p, zl, zh, c)

    def on_y_sib(p):
        return device(x, p, zl, zh, oc)

    def on_z(p):
        return device(x, y, lax.rem(p, 4), p // 4, c)

    def remote(src, dst, ss, rs, to):
        return pltpu.make_async_remote_copy(
            src_ref=src, dst_ref=dst, send_sem=ss, recv_sem=rs, device_id=to, device_id_type=MESH
        )

    def peers(me, size):
        return [(d, lax.rem(me + d, size)) for d in range(1, size)]

    on_x.peers, on_y.peers, on_z.peers = peers(x, 4), peers(y, 4), peers(z, 8)
    zl_peers = peers(zl, 4)

    def on_zl(p):
        return device(x, y, p, zh, c)

    on_zl.peers = zl_peers

    names = (
        "cst", "zst", "xst", "yst", "gain", "near", "zh0", "zh1", "far0", "far1", "sib0", "sib1", "sib2", "wq", "wkv",
        "wo", "qx", "kx", "qz", "kz", "kc", "qy", "a", "b", "c", "e0", "e1", "f", "g",
        "last",
    )
    slot = {name: i for i, name in enumerate(names)}

    def start(name, src, dst, to):
        remote(src, dst, sent.at[slot[name]], come.at[slot[name]], to).start()

    def arrive(name, dst):
        remote(dst, dst, sent.at[slot[name]], come.at[slot[name]], sib).wait_recv()

    def spread(name, src, dst, me, on):
        for _, p in on.peers:
            start(name, src(p), dst.at[me], on(p))

    def collect(name, dst, on):
        arrive(name, dst.at[pl.ds(0, len(on.peers))])

    half = pl.multiple_of(c * HALF, 128)
    other = pl.multiple_of((1 - c) * HALF, 128)
    mine = pl.ds(pl.multiple_of(c * KP, 128), KB)

    def local(src, dst, i):
        return pltpu.make_async_copy(src, dst, lsem.at[i])

    load_x = local(hidden, raw.at[c, n], 0)
    load_x.start()
    load_q = local(query_w.at[:, pl.ds(pl.multiple_of(c * 384, 128), 384)], wq.at[mine], 1)
    load_kv = local(kv_w.at[:, pl.ds(pl.multiple_of(c * 256, 128), 256)], wkv.at[mine], 2)
    load_o = local(out_w, wo.at[c], 3)
    load_k = local(keys_h, keys, 4)
    load_v = local(values_h, values, 5)
    load_q.start()
    load_kv.start()

    barrier = pltpu.get_barrier_semaphore()
    greeted = [on(p) for on in (on_z, on_x, on_y) for _, p in on.peers] + [sib]
    greeted += [on_y_sib(p) for _, p in on_y.peers] + [partner_sib]
    for to in greeted:
        pl.semaphore_signal(barrier, inc=1, device_id=to, device_id_type=MESH)

    for k in range(2):
        pad = pl.ds(k * KP + KB, KP - KB)
        normed[:, pad] = jnp.zeros((512, KP - KB), BF16)
        wq[pad, :] = jnp.zeros((KP - KB, 384), BF16)
        wkv[pad, :] = jnp.zeros((KP - KB, 256), BF16)

        def fill(j, carry, pad=pad):
            wgu[j, pad, :] = jnp.zeros((KP - KB, 2 * CW), BF16)
            return carry

        lax.fori_loop(0, CHUNKS, fill, 0)
    caf[...] = jnp.zeros((2, 32, 256), F32)
    yt[...] = jnp.zeros((2, 4, 8, 384), F32)
    load_x.wait()
    own = raw[c, n].astype(F32)
    row64 = lax.broadcasted_iota(jnp.int32, (64, 128), 0)
    lane = lax.broadcasted_iota(jnp.int32, (64, 128), 1)
    both = jnp.where(
        lane < 64,
        jnp.sum(own, axis=1, keepdims=True),
        jnp.sum(own * own, axis=1, keepdims=True),
    )
    line = jnp.sum(jnp.where((lane & 63) == row64, both, 0.0), axis=0, keepdims=True)
    cst[c] = jnp.broadcast_to(line, (8, 128))
    gains[c] = jnp.broadcast_to(gain[...].reshape(1, KB), (8, KB))

    pl.semaphore_wait(barrier, len(greeted))

    start("cst", cst.at[c], cst.at[c], sib)
    top = [pl.ds(0, 32), pl.ds(32, 32)]
    for i in range(2):
        start(f"zh{i}", raw.at[c, n, top[i]], raw.at[c, n, top[i]], partner)
    for _, p in on_y.peers:
        start("near", raw.at[c, n], raw.at[c, n], on_y(p))
    start("gain", gains.at[c], gains.at[c], sib)
    arrive("cst", cst.at[oc])
    zst[z] = cst[0] + cst[1]
    spread("zst", lambda p: zst.at[z], zst, z, on_z)
    away_q = pl.ds(pl.multiple_of((1 - c) * 384, 128), 384)
    away_kv = pl.ds(pl.multiple_of((1 - c) * 256, 128), 256)
    start("wq", query_w.at[:, away_q], wq.at[mine], sib)
    start("wkv", kv_w.at[:, away_kv], wkv.at[mine], sib)

    def start_weights(j, carry):
        g = j // 3
        for k, weight in enumerate((gate_w, up_w)):
            to = wgu.at[j, mine, pl.ds(k * CW, CW)]
            there = weight.at[:, pl.ds(pl.multiple_of(other + j * CW, 128), CW)]
            remote(there, to, chunk_w.at[0], chunk_w.at[1 + g], sib).start()
            here = weight.at[:, pl.ds(pl.multiple_of(half + j * CW, 128), CW)]
            local(here, to, 6 + g).start()
        return carry

    lax.fori_loop(0, CHUNKS, start_weights, 0)
    start("wo", out_w, wo.at[c], sib)
    load_o.start()
    load_k.start()
    load_v.start()

    far = (1 - zh) * 4 + y
    near4 = pl.ds(zh * 4, 4)
    far4 = pl.ds((1 - zh) * 4, 4)
    collect("zst", zst, on_z)
    upper = lax.broadcasted_iota(jnp.int32, (8, 128), 0) < 4
    xst[x] = jnp.where(
        upper, (zst[0] + zst[1]) + (zst[2] + zst[3]), (zst[4] + zst[5]) + (zst[6] + zst[7])
    )
    spread("xst", lambda p: xst.at[x], xst, x, on_x)
    for i in range(2):
        arrive(f"zh{i}", raw.at[c, far, top[i]])
        for _, p in on_y.peers:
            start(f"far{i}", raw.at[c, far, top[i]], raw.at[c, far, top[i]], on_y(p))
    arrive("near", raw.at[c, pl.ds(0, 3)])
    start("sib0", raw.at[c, near4], raw.at[c, near4], sib)
    collect("xst", xst, on_x)
    yst[y] = (xst[0] + xst[1]) + (xst[2] + xst[3])
    spread("yst", lambda p: yst.at[y], yst, y, on_y)
    def far_rows():
        for i in range(2):
            arrive(f"far{i}", raw.at[c, pl.ds(0, 3), top[i]])
            start(f"sib{i + 1}", raw.at[c, far4, top[i]], raw.at[c, far4, top[i]], sib)
        for i in range(2):
            arrive(f"sib{i + 1}", raw.at[oc, far4, top[i]])

    def norm(i, carry):
        b = lax.rem(i + zh * 4, 8)
        tile = yst[lax.rem(b, 4)]
        stat = jnp.where(b < 4, tile[0:1, :], tile[4:5, :])

        def column(at):
            return jnp.sum(jnp.where(lane == row64 + at, stat, 0.0), axis=1, keepdims=True)

        average = column(0) / D
        variance = column(64) / D - average * average
        scale = lax.rsqrt(variance + EPS)
        rows = pl.ds(pl.multiple_of(b * 64, 64), 64)
        for k in range(2):
            block = (raw[k, b].astype(F32) - average) * scale * gains[k, 0:1, :]
            normed[rows, k * KP : k * KP + KB] = block.astype(BF16)
        return carry

    load_q.wait()
    load_kv.wait()
    arrive("wq", wq.at[mine])
    arrive("wkv", wkv.at[mine])
    for i in range(2):
        if i == 0:
            arrive("gain", gains.at[oc])
            collect("yst", yst, on_y)
            arrive("sib0", raw.at[oc, near4])
        else:
            far_rows()
        lax.fori_loop(4 * i, 4 * i + 4, norm, 0)
        side = zh if i == 0 else 1 - zh
        rows = normed[pl.ds(pl.multiple_of(side * 256, 256), 256), :]
        query = jnp.dot(rows, wq[...], preferred_element_type=F32)
        for zz in range(2):
            for xx in range(4):
                at = zz * 128 + xx * 32
                pq[xx, side * 2 + zz] = query[at : at + 32]
        two = pl.ds(side * 2, 2)
        for _, p in on_x.peers:
            start("qx", pq.at[p, two], rq.at[x, two], on_x(p))
    k64 = lax.broadcasted_iota(jnp.int32, (64, 512), 0)
    r512 = lax.broadcasted_iota(jnp.int32, (64, 512), 1)
    pick = r512 == (k64 >> 1) * 16 + n * 2 + (k64 & 1)
    chosen = jnp.dot(
        jnp.where(pick, 1.0, 0.0).astype(BF16), normed[...], preferred_element_type=F32
    ).astype(BF16)
    kvs[...] = jnp.dot(chosen, wkv[...], preferred_element_type=F32)
    for zz in range(4):
        for xx in range(4):
            at = zz * 16 + xx * 4
            kvp[xx, zz, 0:4, :] = kvs[at : at + 4, 0:128]
            kvp[xx, zz, 4:8, :] = kvs[at : at + 4, 128:256]
    spread("kx", lambda p: kvp.at[p], kvr, x, on_x)

    def part_q1():
        collect("qx", rq, on_x)
        total = pq[x]
        for _, p in on_x.peers:
            total = total + rq[p]
        for zz in range(4):
            for hh in range(2):
                to = hh * 4 + zz
                zq[to, 0:8] = total[zz, hh * 8 : hh * 8 + 8]
                zq[to, 8:16] = total[zz, 16 + hh * 8 : 24 + hh * 8]
        zqr[z] = zq[z]
        spread("qz", lambda p: zq.at[p], zqr, z, on_z)
        collect("kx", kvr, on_x)
        fresh = kvp[x]
        for _, p in on_x.peers:
            fresh = fresh + kvr[p]
        kz[...] = fresh
        spread("kz", lambda p: kz.at[p], kzr, zl, on_zl)

    def part_q2():
        collect("qz", zqr, on_z)
        sums = [(zqr[k] + zqr[k + 1]) + (zqr[k + 2] + zqr[k + 3]) for k in (0, 4)]
        for hh in range(2):
            cx[hh] = sums[hh]
        for cc in range(2):
            for yy in range(4):
                for hh in range(2):
                    at = cc * 8 + yy * 2
                    yt[cc, yy, hh * 2 : hh * 2 + 2, :] = cx[hh, at : at + 2, :]
        here = c * 4 + y
        yr[here] = yt[c, y]
        for _, p in on_y.peers:
            start("qy", yt.at[c, p], yr.at[here], on_y(p))
            start("qy", yt.at[oc, p], yr.at[here], on_y_sib(p))
        start("qy", yt.at[oc, y], yr.at[here], sib)
        collect("kz", kzr, on_zl)
        fresh = kz[zl]
        for _, p in zl_peers:
            fresh = fresh + kzr[p]
        kc[c] = fresh
        start("kc", kc.at[c], kc.at[c], sib)

    def part_q4():
        arrive("kc", kc.at[oc])
        arrive("qy", yr.at[pl.ds(0, 7)])
        for yy in range(4):
            at = yy * 4
            q48[at : at + 4, :] = yr[yy, 0:4, 0:256]
            q48[16 + at : 20 + at, 0:128] = yr[yy, 0:4, 256:384]
            q48[16 + at : 20 + at, 128:256] = yr[4 + yy, 0:4, 0:128]
            q48[32 + at : 36 + at, :] = yr[4 + yy, 0:4, 128:384]
        load_k.wait()
        load_v.wait()
        q = q48[...].astype(BF16)
        factor = 1.0 / 16.0
        first = lax.broadcasted_iota(jnp.int32, (48, 1), 0) % 2 == 0

        def fresh(k):
            tile = kc[k].astype(BF16).astype(F32)
            sides = []
            for at in (0, 4):
                pair = jnp.where(c == 0, tile[at : at + 2], tile[at + 2 : at + 4])
                sides.append(jnp.where(first, pair[0:1, :], pair[1:2, :]))
            return jnp.concatenate(sides, axis=1)

        def scores_of(r):
            return lax.dot_general(q, keys[r], (((1,), (1,)), ((), ())), preferred_element_type=F32)

        scores = jnp.where(first, scores_of(0), scores_of(1)) * factor
        own_score = jnp.sum(q.astype(F32) * fresh(0), axis=1, keepdims=True) * factor
        position = lax.broadcasted_iota(jnp.int32, (48, 384), 1)
        usable = position < jnp.where(first, lengths[0], lengths[1])
        masked = jnp.where(usable, scores, -1e30)
        highest = jnp.maximum(jnp.max(masked, axis=1, keepdims=True), own_score)
        exps = jnp.where(usable, jnp.exp(masked - highest), 0.0)
        own_exp = jnp.exp(own_score - highest)
        denominator = jnp.sum(exps, axis=1, keepdims=True) + own_exp
        weights = (exps / denominator).astype(BF16)
        own_weight = (own_exp / denominator).astype(BF16).astype(F32)

        def mixed(r):
            return jnp.dot(weights, values[r], preferred_element_type=F32)

        context = jnp.where(first, mixed(0), mixed(1)) + own_weight * fresh(1)
        ctx[...] = context
        for t in range(3):
            for yy in range(4):
                for hh in range(2):
                    at = t * 16 + yy * 4 + hh * 2
                    caf[hh, yy * 8 + t * 2 : yy * 8 + t * 2 + 2, :] = ctx[at : at + 2, :]
        ca[...] = caf[...].astype(BF16)
        ar[z] = ca[zh]
        spread("a", lambda p: ca.at[p // 4], ar, z, on_z)

    def part_c1():
        collect("a", ar, on_z)
        for yy in range(4):
            bs[yy] = ar[:, yy * 8 : yy * 8 + 8, :].astype(F32).reshape(64, 256).astype(BF16)
        br[y] = bs[y]
        spread("b", lambda p: bs.at[p], br, y, on_y)

    def part_c2():
        collect("b", br, on_y)
        brf[...] = br[...].astype(F32)
        for t in range(3):
            for zz in range(4):
                for hh in range(2):
                    for yy in range(4):
                        to = zz * 16 + hh * 8 + yy * 2
                        at = (hh * 4 + zz) * 8 + t * 2
                        ctf[to : to + 2, t * 256 : t * 256 + 256] = brf[yy, at : at + 2, :]
        ct[x] = ctf[...].astype(BF16)
        for _, p in on_x.peers:
            start("c", ct.at[x], ct.at[x], on_x(p))

    def part_c4():
        load_o.wait()
        arrive("wo", wo.at[oc])
        collect("c", ct, on_x)
        for cc in range(2):
            out = lax.dot_general(
                ct[...].reshape(256, 768),
                wo[cc],
                (((1,), (1,)), ((), ())),
                preferred_element_type=F32,
            )
            for xx in range(4):
                for zz in range(4):
                    at = xx * 64 + zz * 16
                    to = (xx % 2) * 16
                    i = jnp.where(zh == zz // 2, 1, 0)
                    block = out[at : at + 16].astype(BF16)
                    os_[i, (zz % 2) * 2 + xx // 2, cc, to : to + 16, :] = block
        for i in range(2):
            spread(f"e{i}", lambda p, i=i: os_.at[i, p], or_.at[i], y, on_y)

    def summed(i):
        collect(f"e{i}", or_.at[i], on_y)
        total = os_[i, y].astype(F32)
        for _, p in on_y.peers:
            total = total + or_[i, p].astype(F32)
        return total

    def part_c5():
        fs[...] = summed(0).astype(BF16)
        start("f", fs.at[c], fr.at[0], partner)
        start("f", fs.at[oc], fr.at[1], partner_sib)
        vf[...] = summed(1)
        gs[...] = vf[oc].astype(BF16)
        start("g", gs, gr, sib)

    right, left = lax.rem(x + 1, 4), lax.rem(x + 3, 4)
    across = lax.rem(x + 2, 4)

    def first_copies(j):
        for k, to in enumerate((right, left)):
            src = part.at[j, :, across, :, pl.ds(k * CW, CW)]
            remote(src, r1.at[j, k], chunk_1.at[0], chunk_1.at[1 + j], on_x(to)).start()

    def came(sems, j, dst):
        remote(dst, dst, sems.at[0], sems.at[1 + j], sib).wait_recv()

    def z_first(j):
        return functools.reduce(jnp.logical_or, [j == b for b in Z_FIRST])

    def z_index(j):
        return sum([jnp.where(j > b, 1, 0) for b in Z_FIRST[:-1]], 0)

    def multiply(j):
        def ready():
            three = pl.ds(j, 3)
            to = wgu.at[three, mine]
            local(to, to, 6 + j // 3).wait()
            remote(to, to, chunk_w.at[0], chunk_w.at[1 + j // 3], sib).wait_recv()

        pl.when(lax.rem(j, 3) == 0)(ready)
        product = jnp.dot(normed[...], wgu[j], preferred_element_type=F32)
        part[j] = product.astype(BF16).reshape(4, 4, 32, 2 * CW)

        @pl.when(jnp.logical_not(z_first(j)))
        def _():
            first_copies(j)

        @pl.when(z_first(j))
        def _():
            for _, p in zl_peers:
                to = zb.at[z_index(j), zl]
                remote(part.at[j, p], to, chunk_1.at[0], chunk_1.at[1 + j], on_zl(p)).start()

    def add_first(j):
        came(chunk_1, j, r1.at[j])
        for k, to in enumerate((right, left)):
            for m in range(2):
                cols = slice(m * CW, m * CW + CW)
                if m == k:
                    total = part[j, :, to, :, cols].astype(F32) + r1[j, k].astype(F32)
                    s1[j, k, :, :, cols] = total.astype(BF16)
                else:
                    s1[j, k, :, :, cols] = part[j, :, to, :, cols]
            remote(s1.at[j, k], r2.at[j, k], chunk_2.at[0], chunk_2.at[1 + j], on_x(to)).start()

    def add_second(j):
        came(chunk_2, j, r2.at[j])
        total = part[j, :, x].astype(F32) + r2[j, 0].astype(F32) + r2[j, 1].astype(F32)
        zs[j] = total.astype(BF16)
        for _, p in zl_peers:
            remote(zs.at[j, p], zr.at[j, zl], chunk_3.at[0], chunk_3.at[1 + j], on_zl(p)).start()

    def add_z(j):
        i = z_index(j)
        came(chunk_1, j, zb.at[i, pl.ds(0, 3)])
        total = part[j, zl].astype(F32)
        for _, p in zl_peers:
            total = total + zb[i, p].astype(F32)
        xs[i] = total.astype(BF16)
        for _, p in on_x.peers:
            remote(xs.at[i, p], xr.at[i, x], chunk_2.at[0], chunk_2.at[1 + j], on_x(p)).start()

    def gated(j, total):
        g = total[:, :CW]
        hidden_units = (g * (1.0 / (1.0 + jnp.exp(-g))) * total[:, CW:]).astype(BF16)
        sl[j] = hidden_units.reshape(2, 16, CW)
        start("last", sl.at[j, 1 - c], sr.at[j], sib)
        slab[:, pl.ds(pl.multiple_of(half + j * CW, 128), CW)] = sl[j, c]

    def finish(j):
        came(chunk_3, j, zr.at[j, pl.ds(0, 3)])
        total = zs[j, zl].astype(F32)
        for _, p in zl_peers:
            total = total + zr[j, p].astype(F32)
        gated(j, total)

    def finish_z(j):
        i = z_index(j)
        came(chunk_2, j, xr.at[i, pl.ds(0, 3)])
        total = xs[i, x].astype(F32)
        for _, p in on_x.peers:
            total = total + xr[i, p].astype(F32)
        gated(j, total)

    parts = dict(
        Q1=part_q1, Q2=part_q2, Q4=part_q4, C1=part_c1, C2=part_c2, C4=part_c4, C5=part_c5
    )

    def step(k, carry):
        for name, run in parts.items():
            pl.when(k == STEP[name])(run)
        for lag, run, z_kind in (
            (0, multiply, None),
            (LAG1, add_first, False),
            (LAG3, finish, False),
            (Z_LAG2, finish_z, True),
            (LAG2, add_second, False),
            (Z_LAG1, add_z, True),
        ):
            j = k - lag
            due = jnp.logical_and(j >= 0, j < CHUNKS)
            if z_kind is not None:
                due = jnp.logical_and(due, z_first(j) == z_kind)
            pl.when(due)(functools.partial(run, j))
        return carry

    lax.fori_loop(0, STEPS, step, 0)

    arrive("last", sr)

    def rest(j, carry):
        slab[:, pl.ds(pl.multiple_of(other + j * CW, 128), CW)] = sr[j]
        return carry

    lax.fori_loop(0, CHUNKS, rest, 0)
    arrive("f", fr)
    arrive("g", gr)
    for core, total in ((c, vf[c] + fr[0].astype(F32)), (oc, gr[...].astype(F32) + fr[1].astype(F32))):
        for xx in range(2):
            rows = pl.ds(pl.multiple_of(xx * 32 + core * 16, 16), 16)
            update[rows, :] = total[xx * 16 : xx * 16 + 16].astype(BF16)

    of3, of7 = pl.ds(0, 3), pl.ds(0, 7)
    left_bytes = dict(
        cst=cst.at[0], zst=zst.at[of7], xst=xst.at[of3], yst=yst.at[of3], gain=gains.at[0],
        near=raw.at[0, of3], zh0=raw.at[0, 0, top[0]], zh1=raw.at[0, 0, top[0]],
        far0=raw.at[0, of3, top[0]], far1=raw.at[0, of3, top[0]], sib0=raw.at[0, pl.ds(0, 4)],
        sib1=raw.at[0, pl.ds(0, 4), top[0]], sib2=raw.at[0, pl.ds(0, 4), top[0]], wq=wq.at[pl.ds(0, KB)], wkv=wkv.at[pl.ds(0, KB)],
        qx=rq.at[of3], kx=kvr.at[of3], qz=zqr.at[of7], kz=kzr.at[of3], kc=kc.at[0], wo=wo.at[0],
        qy=yr.at[of7], a=ar.at[of7], b=br.at[of3], c=ct.at[of3],
        e0=or_.at[0, of3], e1=or_.at[1, of3], f=fr, g=gr, last=sr,
    )
    for name, dst in left_bytes.items():
        remote(dst, dst, sent.at[slot[name]], come.at[slot[name]], sib).wait_send()

    def gone(sems, dst):
        remote(dst, dst, sems.at[0], sems.at[1], sib).wait_send()

    a_kind, b_kind = pl.ds(0, CHUNKS - len(Z_FIRST)), pl.ds(0, len(Z_FIRST))
    gone(chunk_w, wgu.at[:, mine])
    gone(chunk_1, r1.at[a_kind])
    gone(chunk_1, zb.at[:, pl.ds(0, 3)])
    gone(chunk_2, r2.at[a_kind])
    gone(chunk_2, xr.at[:, pl.ds(0, 3)])
    gone(chunk_3, zr.at[a_kind, pl.ds(0, 3)])


def scratch():
    v = pltpu.VMEM
    z_chunks = len(Z_FIRST)
    buffers = [
        v((2, 8, 64, KB), BF16),
        v((512, 2 * KP), BF16),
        v((2, 8, KB), F32),
        v((CHUNKS, 2 * KP, 2 * CW), BF16),
        v((2 * KP, 384), BF16),
        v((2 * KP, 256), BF16),
        v((2, KB, 768), BF16),
        v((2, 384, 256), BF16),
        v((2, 384, 256), BF16),
        v((2, 8, 128), F32),
        v((8, 8, 128), F32),
        v((4, 8, 128), F32),
        v((4, 8, 128), F32),
        v((CHUNKS, 4, 4, 32, 2 * CW), BF16),
        v((CHUNKS, 2, 4, 32, CW), BF16),
        v((CHUNKS, 2, 4, 32, 2 * CW), BF16),
        v((CHUNKS, 2, 4, 32, 2 * CW), BF16),
        v((CHUNKS, 4, 32, 2 * CW), BF16),
        v((CHUNKS, 4, 32, 2 * CW), BF16),
        v((z_chunks, 4, 4, 32, 2 * CW), BF16),
        v((z_chunks, 4, 32, 2 * CW), BF16),
        v((z_chunks, 4, 32, 2 * CW), BF16),
        v((CHUNKS, 2, 16, CW), BF16),
        v((CHUNKS, 16, CW), BF16),
        v((64, 256), F32),
        v((4, 4, 8, 128), F32),
        v((4, 4, 8, 128), F32),
        v((4, 8, 128), F32),
        v((4, 8, 128), F32),
        v((2, 8, 128), F32),
        v((4, 4, 32, 384), F32),
        v((4, 4, 32, 384), F32),
        v((8, 16, 384), F32),
        v((8, 16, 384), F32),
        v((2, 16, 384), F32),
        v((2, 4, 8, 384), F32),
        v((8, 8, 384), F32),
        v((48, 256), F32),
        v((48, 256), F32),
        v((2, 32, 256), F32),
        v((2, 32, 256), BF16),
        v((8, 32, 256), BF16),
        v((4, 64, 256), BF16),
        v((4, 64, 256), BF16),
        v((4, 64, 256), F32),
        v((64, 768), F32),
        v((4, 64, 768), BF16),
        v((2, 4, 2, 32, KB), BF16),
        v((2, 4, 2, 32, KB), BF16),
        v((2, 32, KB), F32),
        v((2, 32, KB), BF16),
        v((2, 32, KB), BF16),
        v((32, KB), BF16),
        v((32, KB), BF16),
    ]
    counts = (9, 30, 30, 4, 1 + CHUNKS, 1 + CHUNKS, 1 + CHUNKS)
    return buffers + [pltpu.SemaphoreType.DMA((count,)) for count in counts]


def copy_out(update, slab, update_out, slab_out):
    update_out[...] = update[...]
    slab_out[...] = slab[...]


def local(hidden, gain, gate_w, up_w, query_w, kv_w, out_w, *rest):
    anywhere = pl.BlockSpec(memory_space=pl.ANY)
    vmem = pl.BlockSpec(memory_space=pltpu.VMEM)
    shapes = (
        jax.ShapeDtypeStruct((64, KB), BF16),
        jax.ShapeDtypeStruct((16, 2 * HALF), BF16),
    )
    results = pl.pallas_call(
        kernel,
        out_shape=shapes,
        in_specs=[anywhere, vmem] + [anywhere] * 7 + [pl.BlockSpec(memory_space=pltpu.SMEM)],
        out_specs=(vmem, vmem),
        scratch_shapes=scratch(),
        compiler_params=pltpu.CompilerParams(
            collective_id=0, has_side_effects=True, vmem_limit_bytes=58 * 1024 * 1024
        ),
        name="layer",
    )(hidden, gain, gate_w, up_w, query_w, kv_w, out_w.T, *rest)
    return pl.pallas_call(
        copy_out,
        out_shape=shapes,
        in_specs=[vmem, vmem],
        out_specs=(vmem, vmem),
        name="outputs",
    )(*results)


def solution(mesh):
    placed = (
        P("narrow", "wide"),
        P("wide"),
        P("wide", "narrow"),
        P("wide", "narrow"),
        P("wide", "narrow"),
        P("wide", None),
        P("narrow", "wide"),
        P(("wide", "narrow"), None, None),
        P(("wide", "narrow"), None, None),
        P(("wide", "narrow")),
    )
    return jax.shard_map(
        local,
        mesh=mesh,
        in_specs=placed,
        out_specs=(P("narrow", "wide"), P("wide", "narrow")),
        check_vma=False,
    )
```
